32 devices in a mesh: shard: 2 (over x), ctx: 4 (over y, core), tensor: 4 (over z).
Axes of the slice: x: 2, y: 2, z: 4, core: 2. Of those that a mesh axis runs over, the one named last changes fastest.
Arguments:
- inputs: bfloat16 [1024, 4, 1024], P('ctx', 'shard', 'tensor'), may hold values from -6 to 6
- w_query: bfloat16 [2, 1024, 1024], P(None, ('shard', 'ctx'), 'tensor'), may hold values from -0.1875 to 0.1875
- w_key: bfloat16 [2, 1024, 1024], P(None, ('shard', 'ctx'), 'tensor'), may hold values from -0.1875 to 0.1875
- w_value: bfloat16 [2, 1024, 1024], P(None, ('shard', 'ctx'), 'tensor'), may hold values from -0.1875 to 0.1875
- w_out: bfloat16 [2, 1024, 1024], P(None, 'tensor', ('shard', 'ctx')), may hold values from -3 to 3
- w_gate: bfloat16 [2, 1024, 4096], P(None, ('shard', 'ctx'), 'tensor'), may hold values from -0.1875 to 0.1875
- w_up: bfloat16 [2, 1024, 4096], P(None, ('shard', 'ctx'), 'tensor'), may hold values from -0.1875 to 0.1875
- w_down: bfloat16 [2, 4096, 1024], P(None, 'tensor', ('shard', 'ctx')), may hold values from -0.09375 to 0.09375
- attn_gain: float32 [2, 1024], P(None, 'tensor'), may hold values from 0.5 to 1.5
- ffn_gain: float32 [2, 1024], P(None, 'tensor'), may hold values from 0.5 to 1.5
- variate_bias: float32 [2, 16, 2], P(None, 'tensor'), may hold values from -4 to 4
- lengths: int32 [4], P('shard'), may hold values from 512 to 1024, as said below
- variates: int32 [1024, 4], P('ctx', 'shard'), may hold values from 0 to 7
- cotangent: bfloat16 [1024, 4, 1024], P('ctx', 'shard', 'tensor'), may hold values from -6 to 6
Outputs:
- output: bfloat16 [1024, 4, 1024], P('ctx', 'shard', 'tensor')
- input_grad: float32 [1024, 4, 1024], P('ctx', 'shard', 'tensor')
- grad_w_query: float32 [2, 1024, 1024], P(None, ('shard', 'ctx'), 'tensor')
- grad_w_key: float32 [2, 1024, 1024], P(None, ('shard', 'ctx'), 'tensor')
- grad_w_value: float32 [2, 1024, 1024], P(None, ('shard', 'ctx'), 'tensor')
- grad_w_out: float32 [2, 1024, 1024], P(None, 'tensor', ('shard', 'ctx'))
- grad_w_gate: float32 [2, 1024, 4096], P(None, ('shard', 'ctx'), 'tensor')
- grad_w_up: float32 [2, 1024, 4096], P(None, ('shard', 'ctx'), 'tensor')
- grad_w_down: float32 [2, 4096, 1024], P(None, 'tensor', ('shard', 'ctx'))
- grad_attn_gain: float32 [2, 1024], P(None, 'tensor')
- grad_ffn_gain: float32 [2, 1024], P(None, 'tensor')
- grad_variate_bias: float32 [2, 16, 2], P(None, 'tensor')
The draws below stay inside these ranges and needn't reach their ends.
Inputs may be any that keep to these rules, and one draw needn't show every extreme that they name: `lengths`: of every 2 consecutive slots (those of one index of shard), one, drawn from the seed, has length 1024.
All inputs are finite; a program needn't handle non-finite values.
Results may differ from the reference program's by a relative error of at most 0.034.
Values may be sent and summed in bfloat16 or wider, within the bound.
No kernel may reach another device: no remote copies, remote signals or barrier semaphores. Data moves between devices by JAX's collectives and lax.ppermute only.
A program may use at most 192 MiB of HBM per device.

```python
from functools import partial
import jax
import jax.numpy as jnp
from jax import lax

D = 1024
H = 16
HD = 64
FF = 4096
SLOT_LEN = 1024
LAYERS = 2
VARS = 8
SLOTS = 2
SLOTS_ALL = 4
MIN_LEN = 512


def draw_lengths(key, part):
    key = jax.random.fold_in(key, 7)
    key_lengths, key_choice = jax.random.split(key)
    groups = SLOTS_ALL // SLOTS
    drawn_lengths = jax.random.randint(key_lengths, (groups, SLOTS), MIN_LEN, SLOT_LEN + 1)
    chosen = jax.random.randint(key_choice, (groups, 1), 0, SLOTS)
    longest = jnp.arange(SLOTS)[None, :] == chosen
    return jnp.where(longest, SLOT_LEN, drawn_lengths).reshape(SLOTS_ALL).astype(jnp.int32)


def touch_ends(result, own_key, least, largest):
    dims = result.shape
    spot = [jax.random.randint(jax.random.fold_in(own_key, axis), (), 0, dims[axis]) for axis in range(len(dims))]
    result = result.at[tuple(spot)].set(least)
    longest = dims.index(max(dims))
    spot[longest] = (spot[longest] + 1) % dims[longest]
    return result.at[tuple(spot)].set(largest)


def level_of(key, dims, cuts, low, top_value):
    def one(axis_at, shards_of):
        heights = jax.random.uniform(jax.random.fold_in(jax.random.fold_in(key, 6), axis_at), (shards_of,), jnp.float32, low / len(cuts), top_value / len(cuts))
        return jnp.repeat(jnp.exp(heights), dims[axis_at] // shards_of).reshape((-1,) + (1,) * (len(dims) - axis_at - 1))

    level = one(*cuts[0])
    for cut in cuts[1:]:
        level = level * one(*cut)
    return level


def gaussian(rng, dims, deviation, reach, cuts=(), held_as=jnp.bfloat16):
    level = level_of(rng, dims, cuts, -0.22, 0.18) if cuts else 1.0
    result = jax.random.normal(rng, dims, jnp.float32) * deviation * level
    return jnp.minimum(jnp.maximum(result, -reach), reach).astype(held_as)


def setup_inputs(seed: int = 0) -> dict:
    splits = jax.random.split(jax.random.key(seed), 15)
    return {
        "inputs": gaussian(splits[0], (SLOT_LEN, SLOTS_ALL, D), 1.0, 6.0, ((0, 4), (1, 2), (2, 4))),
        "w_query": gaussian(splits[1], (LAYERS, D, D), D ** -0.5, 0.1875, ((1, 8), (2, 4))),
        "w_key": gaussian(splits[2], (LAYERS, D, D), D ** -0.5, 0.1875, ((1, 8), (2, 4))),
        "w_value": gaussian(splits[3], (LAYERS, D, D), D ** -0.5, 0.1875, ((1, 8), (2, 4))),
        "w_out": gaussian(splits[4], (LAYERS, D, D), (max(D // 256, 1)) ** -0.5, 3.0, ((1, 4), (2, 8))),
        "w_gate": gaussian(splits[5], (LAYERS, D, FF), D ** -0.5, 0.1875, ((1, 8), (2, 4))),
        "w_up": gaussian(splits[6], (LAYERS, D, FF), D ** -0.5, 0.1875, ((1, 8), (2, 4))),
        "w_down": gaussian(splits[7], (LAYERS, FF, D), FF ** -0.5, 0.09375, ((1, 4), (2, 8))),
        "attn_gain": jnp.clip(1.0 + 0.1 * jax.random.normal(splits[8], (LAYERS, D), jnp.float32), 0.5, 1.5),
        "ffn_gain": jnp.clip(1.0 + 0.1 * jax.random.normal(splits[9], (LAYERS, D), jnp.float32), 0.5, 1.5),
        "variate_bias": gaussian(splits[10], (LAYERS, H, 2), 1.0, 4.0, ((1, 4),), jnp.float32),
        "lengths": draw_lengths(jax.random.fold_in(splits[14], 71), 0),
        "variates": touch_ends(jax.random.randint(splits[12], (SLOT_LEN, SLOTS_ALL), 0, VARS), jax.random.fold_in(splits[12], 1), 0, VARS - 1).astype(jnp.int32),
        "cotangent": gaussian(splits[13], (SLOT_LEN, SLOTS_ALL, D), 1.0, 6.0, ((0, 4), (1, 2), (2, 4))),
    }


epsilon = 1e-06
masked = -1e+30

@jax.custom_vjp
def low(v):
    return lax.optimization_barrier(v.astype(jnp.bfloat16)).astype(jnp.float32)

@jax.custom_vjp
def low_back(v):
    return v

def low_keep(v):
    return (low(v), None)

def low_pass(kept, grad):
    return (grad,)

def back_keep(v):
    return (v, None)

def back_low(kept, grad):
    return (low(grad),)
low.defvjp(low_keep, low_pass)
low_back.defvjp(back_keep, back_low)

def project(values_in, matrix):
    return jnp.einsum('tsd,de->tse', values_in, matrix, precision=lax.Precision.HIGHEST)

def angle_table(positions, half_width):
    index_half = jnp.arange(half_width, dtype=jnp.float32)
    inverse = 10000.0 ** (-(2.0 * index_half) / (2 * half_width))
    return positions.astype(jnp.float32)[:, None] * inverse[None, :]

def rotate(values_in, cosine, sine_table, head_count):
    leading = values_in.shape[:-1]
    width_all = values_in.shape[-1]
    by_head = values_in.reshape(leading + (head_count, width_all // head_count))
    half_width = width_all // head_count // 2
    first_half = by_head[..., :half_width]
    second_half = by_head[..., half_width:]
    cosine = cosine[:, None, None, :]
    sine_table = sine_table[:, None, None, :]
    turned = jnp.concatenate([first_half * cosine - second_half * sine_table, second_half * cosine + first_half * sine_table], axis=-1)
    return turned.reshape(leading + (width_all,))

def rms_norm(values_in, gain_row):
    row_scale = lax.rsqrt(lax.optimization_barrier(jnp.mean(values_in * values_in, axis=-1, keepdims=True)) + epsilon)
    return values_in * row_scale * gain_row

def slot_attention(carried, bias_layer):
    queries, key_rows, values, kind_ids, length = carried
    raw_scores = low_back(jnp.einsum('thd,uhd->htu', queries, key_rows, precision=lax.Precision.HIGHEST) * 0.125)
    same_kind = kind_ids[:, None] == kind_ids[None, :]
    shifted = raw_scores + jnp.where(same_kind[None], bias_layer[:, 0][:, None, None], bias_layer[:, 1][:, None, None])
    key_valid = jnp.arange(SLOT_LEN) < length
    shifted = jnp.where(key_valid[None, None, :], shifted, masked)
    soft_weights = jax.nn.softmax(shifted, axis=-1)
    return jnp.einsum('htu,uhd->thd', low(soft_weights), values, precision=lax.Precision.HIGHEST)

def forward(inputs, w_query, w_key, w_value, w_out, w_gate, w_up, w_down, attn_gain, ffn_gain, variate_bias, lengths, variates):
    positions = jnp.arange(SLOT_LEN)
    angles = angle_table(positions, HD // 2)
    cosine = jnp.cos(angles)
    sine_table = jnp.sin(angles)
    slot_total = inputs.shape[1]
    current = inputs
    for layer_index in range(LAYERS):
        normed = low(rms_norm(current, attn_gain[layer_index]))
        queries = low(rotate(low_back(project(normed, w_query[layer_index])), cosine, sine_table, H))
        key_rows = low(rotate(low_back(project(normed, w_key[layer_index])), cosine, sine_table, H))
        values = low(low_back(project(normed, w_value[layer_index])))
        per_slot = (queries.reshape(SLOT_LEN, slot_total, H, HD).transpose(1, 0, 2, 3), key_rows.reshape(SLOT_LEN, slot_total, H, HD).transpose(1, 0, 2, 3), values.reshape(SLOT_LEN, slot_total, H, HD).transpose(1, 0, 2, 3), variates.T, lengths)
        attended = lax.map(jax.checkpoint(partial(slot_attention, bias_layer=variate_bias[layer_index])), per_slot)
        attended = attended.transpose(1, 0, 2, 3).reshape(SLOT_LEN, slot_total, D)
        attended = low_back(low(attended))
        current = current + low_back(project(attended, w_out[layer_index]))
        normed_ffn = low(rms_norm(current, ffn_gain[layer_index]))
        gate_pre = low_back(project(normed_ffn, w_gate[layer_index]))
        up_pre = low_back(project(normed_ffn, w_up[layer_index]))
        hidden = low(jax.nn.silu(gate_pre) * up_pre)
        current = current + low_back(project(hidden, w_down[layer_index]))
    valid_rows = (positions[:, None] < lengths[None, :]).astype(jnp.float32)
    return current * valid_rows[:, :, None]

def reference(inputs, w_query, w_key, w_value, w_out, w_gate, w_up, w_down, attn_gain, ffn_gain, variate_bias, lengths, variates, cotangent):
    floats = [array.astype(jnp.float32) for array in (inputs, w_query, w_key, w_value, w_out, w_gate, w_up, w_down, attn_gain, ffn_gain, variate_bias)]

    def closed(*params):
        return forward(*params, lengths, variates)
    output, pullback = jax.vjp(closed, *floats)
    gradients = pullback(cotangent.astype(jnp.float32))
    return (output.astype(jnp.bfloat16), gradients[0], gradients[1], gradients[2], gradients[3], gradients[4], gradients[5], gradients[6], gradients[7], gradients[8], gradients[9], gradients[10])
```

```python
import jax
import jax.numpy as jnp
from jax import lax
from jax.sharding import PartitionSpec as P

HD = 64
LAYERS = 2
epsilon = 1e-06
masked = -1e30
F32 = jnp.float32
LOW = jnp.bfloat16
AXES = ("shard", "ctx", "tensor")


def bits_of(count):
    width = count.bit_length() - 1
    assert 1 << width == count
    return width


def dot(left, right, left_dim, right_dim):
    return lax.dot_general(
        left, right, (((left_dim,), (right_dim,)), ((), ())), preferred_element_type=F32
    )


class Place:
    def __init__(self, mesh):
        self.n_shard = mesh.shape["shard"]
        self.n_ctx = mesh.shape["ctx"]
        assert mesh.shape["tensor"] == 4 and self.n_ctx % 2 == 0
        self.s_bits = bits_of(self.n_shard)
        self.o_bits = bits_of(self.n_ctx // 2)
        self.dp = [("s", i) for i in reversed(range(self.s_bits))] + [
            ("o", i) for i in reversed(range(self.o_bits))
        ]

    def locate(self):
        shard = lax.axis_index("shard")
        ctx = lax.axis_index("ctx")
        tensor = lax.axis_index("tensor")
        self.o = ctx // 2
        self.c = ctx % 2
        self.zh = tensor // 2
        self.zl = tensor % 2
        self.dp_bit = [((shard if kind == "s" else self.o) >> i) & 1 for kind, i in self.dp]

    def move(self, array, route):
        pairs = []
        for shard in range(self.n_shard):
            for ctx in range(self.n_ctx):
                for tensor in range(4):
                    s, o, c, zh, zl = route(shard, ctx // 2, ctx % 2, tensor // 2, tensor % 2)
                    source = (shard * self.n_ctx + ctx) * 4 + tensor
                    target = (s * self.n_ctx + 2 * o + c) * 4 + 2 * zh + zl
                    pairs.append((source, target))
        return lax.ppermute(array, AXES, pairs)

    def swap_core(self, array):
        return self.move(array, lambda s, o, c, zh, zl: (s, o, 1 - c, zh, zl))

    def swap_zl(self, array):
        return self.move(array, lambda s, o, c, zh, zl: (s, o, c, zh, 1 - zl))

    def swap_zh(self, array):
        return self.move(array, lambda s, o, c, zh, zl: (s, o, c, 1 - zh, zl))

    def swap_dp(self, array, index):
        kind, i = self.dp[index]
        if kind == "s":
            return self.move(array, lambda s, o, c, zh, zl: (s ^ (1 << i), o, c, zh, zl))
        return self.move(array, lambda s, o, c, zh, zl: (s, o ^ (1 << i), c, zh, zl))

    def near(self, array):
        return self.move(array, lambda s, o, c, zh, zl: (s, o, zh, c, zl))

    def far(self, array):
        return self.move(array, lambda s, o, c, zh, zl: (s, o, zh, 1 - c, zl))

    def far_back(self, array):
        return self.move(array, lambda s, o, c, zh, zl: (s, o, 1 - zh, c, zl))


def flip_if(bit, array, axis):
    return jnp.where(bit == 1, jnp.flip(array, axis), array)


def pick(flag, one, two):
    return jnp.where(flag == 1, one, two)


def to_frame(place, rows):
    lead = rows.shape[:-1]
    k = len(place.dp)
    blocks = 2 ** (k + 1)
    width = rows.shape[-1] // blocks
    cut = rows.reshape(lead + (2,) * (k + 1) + (width,))
    n = len(lead)
    for i in range(k):
        cut = flip_if(place.dp_bit[i], cut, n + i)
    cut = flip_if(place.zh, cut, n + k)
    first = lax.index_in_dim(cut, 0, n + k, keepdims=False)
    second = lax.index_in_dim(cut, 1, n + k, keepdims=False)
    order = tuple(range(n)) + tuple(reversed(range(n, n + k))) + (n + k,)
    second = second.transpose(order)
    half = rows.shape[-1] // 2
    return jnp.concatenate([first.reshape(lead + (half,)), second.reshape(lead + (half,))], -1)


def from_frame(place, rows):
    lead = rows.shape[:-1]
    k = len(place.dp)
    blocks = 2 ** (k + 1)
    width = rows.shape[-1] // blocks
    n = len(lead)
    half = rows.shape[-1] // 2
    first = rows[..., :half].reshape(lead + (2,) * k + (width,))
    second = rows[..., half:].reshape(lead + (2,) * k + (width,))
    order = tuple(range(n)) + tuple(reversed(range(n, n + k))) + (n + k,)
    second = second.transpose(order)
    cut = jnp.stack([first, second], n + k)
    for i in range(k):
        cut = flip_if(place.dp_bit[i], cut, n + i)
    cut = flip_if(place.zh, cut, n + k)
    return cut.reshape(lead + (rows.shape[-1],))


def gather_rows(place, natural):
    k = len(place.dp)
    halves = []
    for part, order in ((place.near(natural), range(k)), (place.far(natural), reversed(range(k)))):
        pieces = [part]
        for index in order:
            received = [place.swap_dp(piece, index) for piece in pieces]
            pieces = [piece for pair in zip(pieces, received) for piece in pair]
        halves += pieces
    return jnp.concatenate(halves, 0)


def scatter_rows(place, partial):
    k = len(place.dp)
    half = partial.shape[0] // 2
    ends = []
    for part, order in ((partial[:half], range(k)), (partial[half:], reversed(range(k)))):
        for index in order:
            middle = part.shape[0] // 2
            received = place.swap_dp(part[middle:], index)
            part = (part[:middle].astype(F32) + received.astype(F32)).astype(LOW)
        ends.append(part)
    return place.near(ends[0]).astype(F32) + place.far_back(ends[1]).astype(F32)


def gather_feats(place, share):
    other = place.swap_zl(share)
    half = jnp.concatenate([pick(place.zl, other, share), pick(place.zl, share, other)], -1)
    rest = place.swap_core(half)
    return jnp.concatenate([pick(place.c, rest, half), pick(place.c, half, rest)], -1)


def scatter_feats(place, partial):
    wide = partial.shape[-1] // 2
    first, second = partial[:, :wide], partial[:, wide:]
    received = place.swap_core(pick(place.c, first, second).astype(LOW))
    kept = pick(place.c, second, first) + received.astype(F32)
    width = wide // 2
    first, second = kept[:, :width], kept[:, width:]
    received = place.swap_zl(pick(place.zl, first, second).astype(LOW))
    return pick(place.zl, second, first) + received.astype(F32)


def gather_tokens(place, natural):
    positions, slots, width = natural.shape
    half = slots // 2
    first, second = natural[:, :half], natural[:, half:]
    received = place.swap_zh(pick(place.zh, first, second))
    own = pick(place.zh, second, first)
    two = jnp.stack([pick(place.zh, received, own), pick(place.zh, own, received)], 2)
    other = place.swap_zl(two)
    four = jnp.stack([pick(place.zl, other, two), pick(place.zl, two, other)], 3)
    full = four.reshape(positions, half, 4 * width).transpose(1, 0, 2)
    rest = place.swap_core(full)
    both = jnp.concatenate([pick(place.c, rest, full), pick(place.c, full, rest)], 1)
    return to_frame(place, both.reshape(half * 2 * positions, 4 * width))


def place_tokens(place, rows, positions, slots):
    half = slots // 2
    width = rows.shape[-1] // 4
    cut = from_frame(place, rows).reshape(half, 2, positions, 2, 2, width)
    cut = pick(place.c, cut[:, 1], cut[:, 0])
    cut = pick(place.zl, cut[:, :, :, 1], cut[:, :, :, 0])
    own = pick(place.zh, cut[:, :, 1], cut[:, :, 0])
    received = place.swap_zh(pick(place.zh, cut[:, :, 0], cut[:, :, 1]))
    both = jnp.concatenate(
        [pick(place.zh, received, own), pick(place.zh, own, received)], 0
    )
    return both.transpose(1, 0, 2)


def gather_keys(place, own):
    pieces = [own]
    for index in reversed(range(place.s_bits, len(place.dp))):
        received = [place.swap_dp(piece, index) for piece in pieces]
        pieces = pieces + received
    return jnp.concatenate(pieces, 1)


def scatter_keys(place, partial):
    for index in range(place.s_bits, len(place.dp)):
        middle = partial.shape[1] // 2
        received = place.swap_dp(partial[:, middle:].astype(LOW), index)
        partial = partial[:, :middle] + received.astype(F32)
    return partial


def rotate(values, cosine, sine):
    lead = values.shape[:-1]
    heads = values.shape[-1] // HD
    cut = values.reshape(lead + (heads, 2, HD // 2))
    first, second = cut[..., 0, :], cut[..., 1, :]
    cosine = cosine[:, None, :]
    sine = sine[:, None, :]
    turned = jnp.stack(
        [first * cosine - second * sine, second * cosine + first * sine], axis=-2
    )
    return turned.reshape(values.shape)


def head_scores(queries, keys, same_kind, key_valid, bias_pair):
    raw = jnp.einsum("scd,sud->scu", queries, keys, preferred_element_type=F32) * 0.125
    shifted = raw + jnp.where(same_kind, bias_pair[0], bias_pair[1])
    return jnp.where(key_valid, shifted, masked)


def attend(queries, keys, values, same_kind, key_valid, bias):
    outputs = []
    logs = []
    for head in range(queries.shape[2] // HD):
        cols = slice(head * HD, (head + 1) * HD)
        scores = head_scores(
            queries[:, :, cols], keys[:, :, cols], same_kind, key_valid, bias[head]
        )
        highest = jnp.max(scores, axis=-1, keepdims=True)
        exponent = jnp.exp(scores - highest)
        totals = jnp.sum(exponent, axis=-1, keepdims=True)
        weights = (exponent / totals).astype(LOW)
        outputs.append(
            jnp.einsum("scu,sud->scd", weights, values[:, :, cols], preferred_element_type=F32)
        )
        logs.append(highest[..., 0] + jnp.log(totals[..., 0]))
    return jnp.concatenate(outputs, axis=-1).astype(LOW), logs


def attend_back(queries, keys, values, same_kind, key_valid, bias, logs, out_grad):
    query_grads, key_grads, value_grads, bias_grads = [], [], [], []
    for head in range(queries.shape[2] // HD):
        cols = slice(head * HD, (head + 1) * HD)
        scores = head_scores(
            queries[:, :, cols], keys[:, :, cols], same_kind, key_valid, bias[head]
        )
        soft = jnp.exp(scores - logs[head][..., None])
        soft_grad = jnp.einsum(
            "scd,sud->scu", out_grad[:, :, cols], values[:, :, cols], preferred_element_type=F32
        )
        weighted = jnp.sum(soft * soft_grad, axis=-1, keepdims=True)
        score_grad = soft * (soft_grad - weighted)
        bias_grads.append(
            jnp.stack(
                [
                    jnp.sum(jnp.where(same_kind, score_grad, 0.0)),
                    jnp.sum(jnp.where(same_kind, 0.0, score_grad)),
                ]
            )
        )
        low = score_grad.astype(LOW)
        query_grads.append(
            jnp.einsum("scu,sud->scd", low, keys[:, :, cols], preferred_element_type=F32) * 0.125
        )
        key_grads.append(
            jnp.einsum("scu,scd->sud", low, queries[:, :, cols], preferred_element_type=F32)
            * 0.125
        )
        value_grads.append(
            jnp.einsum(
                "scu,scd->sud",
                soft.astype(LOW),
                out_grad[:, :, cols],
                preferred_element_type=F32,
            )
        )
    return (
        jnp.concatenate(query_grads, axis=-1),
        jnp.concatenate(key_grads, axis=-1),
        jnp.concatenate(value_grads, axis=-1),
        jnp.stack(bias_grads),
    )


def per_device(place):
    def run(
        inputs,
        w_query,
        w_key,
        w_value,
        w_out,
        w_gate,
        w_up,
        w_down,
        attn_gain,
        ffn_gain,
        variate_bias,
        lengths,
        variates,
        cotangent,
    ):
        place.locate()
        positions, slots, quarter = inputs.shape
        D = quarter * 4
        half_slots = slots // 2
        block = 2 * positions
        n_o = place.n_ctx // 2
        tokens = half_slots * block
        heads = w_query.shape[2] // HD
        own_quarter = 2 * place.c + place.zl

        small = jnp.concatenate(
            [attn_gain.reshape(-1), ffn_gain.reshape(-1), variate_bias.reshape(-1)]
        )
        small = lax.all_gather(small, "tensor", axis=0)
        cut = LAYERS * quarter
        natural_gains = [
            small[:, i * cut : (i + 1) * cut]
            .reshape(4, LAYERS, quarter)
            .transpose(1, 0, 2)
            .reshape(LAYERS, D)
            for i in range(2)
        ]
        attn_gains = to_frame(place, natural_gains[0])
        ffn_gains = to_frame(place, natural_gains[1])
        biases = lax.dynamic_index_in_dim(
            small[:, 2 * cut :].reshape(4, LAYERS, heads, 2), own_quarter, 0, keepdims=False
        )

        kinds = lax.all_gather(variates, "ctx", axis=0)
        kinds = kinds.reshape((2,) * place.o_bits + (block, slots))
        for i in range(place.o_bits):
            kinds = flip_if(place.dp_bit[place.s_bits + i], kinds, i)
        kinds = kinds.reshape(n_o, block, slots)
        kinds = pick(place.zh, kinds[:, :, half_slots:], kinds[:, :, :half_slots])
        kinds = kinds.reshape(n_o * block, half_slots).T
        own_kinds = kinds[:, :block]
        same_kind = own_kinds[:, :, None] == kinds[:, None, :]
        own_lengths = pick(place.zh, lengths[half_slots:], lengths[:half_slots])
        own_positions = place.o * block + jnp.arange(block, dtype=jnp.int32)
        chips = jnp.arange(n_o, dtype=jnp.int32) ^ place.o
        key_positions = (
            chips[:, None] * block + jnp.arange(block, dtype=jnp.int32)[None, :]
        ).reshape(-1)
        key_valid = (key_positions[None, :] < own_lengths[:, None])[:, None, :]
        valid = (own_positions[None, :] < own_lengths[:, None]).astype(F32).reshape(tokens, 1)
        inverse = 10000.0 ** (-(2.0 * jnp.arange(HD // 2, dtype=F32)) / HD)
        angles = own_positions.astype(F32)[:, None] * inverse[None, :]
        cosine, sine = jnp.cos(angles), jnp.sin(angles)

        def share_of(rows):
            return lax.dynamic_slice_in_dim(rows, own_quarter * quarter, quarter, -1)

        full = gather_tokens(place, inputs)
        packed = []
        for layer in range(LAYERS):
            attn_pack = jnp.concatenate(
                [w_query[layer], w_key[layer], w_value[layer], w_out[layer].T], 1
            )
            ffn_pack = jnp.concatenate([w_gate[layer], w_up[layer], w_down[layer].T], 1)
            packed.append((gather_rows(place, attn_pack), gather_rows(place, ffn_pack)))

        current = share_of(full).astype(F32)
        kept = []
        for layer in range(LAYERS):
            attn_w, ffn_w = packed[layer]
            hidden = ffn_w.shape[1] // 3
            width = attn_w.shape[1] // 4
            full_float = full.astype(F32)
            scale = lax.rsqrt(jnp.mean(full_float * full_float, -1, keepdims=True) + epsilon)
            normed = (full_float * scale * attn_gains[layer]).astype(LOW)
            three = dot(normed, attn_w[:, : 3 * width], 1, 0)
            three = three.reshape(half_slots, block, 3 * width)
            queries = rotate(three[:, :, :width], cosine, sine).astype(LOW)
            keys = rotate(three[:, :, width : 2 * width], cosine, sine).astype(LOW)
            values = three[:, :, 2 * width :].astype(LOW)
            both = gather_keys(place, jnp.concatenate([keys, values], -1))
            keys, values = both[:, :, :width], both[:, :, width:]
            attended, logs = attend(queries, keys, values, same_kind, key_valid, biases[layer])
            flat = attended.reshape(tokens, width)
            middle = current + scatter_feats(place, dot(flat, attn_w[:, 3 * width :], 1, 1))
            full_mid = gather_feats(place, middle.astype(LOW))
            mid_float = full_mid.astype(F32)
            scale_mid = lax.rsqrt(jnp.mean(mid_float * mid_float, -1, keepdims=True) + epsilon)
            normed_mid = (mid_float * scale_mid * ffn_gains[layer]).astype(LOW)
            gate_up = dot(normed_mid, ffn_w[:, : 2 * hidden], 1, 0)
            gate, up = gate_up[:, :hidden], gate_up[:, hidden:]
            hid = (jax.nn.silu(gate) * up).astype(LOW)
            current = middle + scatter_feats(place, dot(hid, ffn_w[:, 2 * hidden :], 1, 1))
            kept.append(
                (
                    full,
                    scale,
                    normed,
                    queries,
                    keys,
                    values,
                    attended,
                    logs,
                    full_mid,
                    scale_mid,
                    normed_mid,
                    gate,
                    up,
                    hid,
                )
            )
            full = gather_feats(place, current.astype(LOW))

        output = place_tokens(place, (full * valid.astype(LOW)), positions, slots)

        upstream_full = gather_tokens(place, cotangent) * valid.astype(LOW)
        upstream = share_of(upstream_full).astype(F32)

        def norm_back(partial, full_rows, row_scale, gain, before, before_full):
            shared = scatter_feats(place, partial)
            own_rows = share_of(full_rows).astype(F32) * row_scale
            gain_grad = jnp.sum(shared * own_rows, 0)
            moved = before + row_scale * (shared * share_of(gain))
            moved_full = gather_feats(place, moved.astype(LOW)).astype(F32)
            rows = full_rows.astype(F32) * row_scale
            dots = jnp.sum((moved_full - before_full.astype(F32)) * rows, -1, keepdims=True) / D
            after = moved - own_rows * dots
            after_full = (moved_full - rows * dots).astype(LOW)
            return after, after_full, gain_grad

        weight_grads = [None] * LAYERS
        gain_grads = [None] * LAYERS
        bias_grads = [None] * LAYERS
        for layer in reversed(range(LAYERS)):
            attn_w, ffn_w = packed[layer]
            hidden = ffn_w.shape[1] // 3
            width = attn_w.shape[1] // 4
            (
                full,
                scale,
                normed,
                queries,
                keys,
                values,
                attended,
                logs,
                full_mid,
                scale_mid,
                normed_mid,
                gate,
                up,
                hid,
            ) = kept[layer]
            hid_grad = dot(upstream_full, ffn_w[:, 2 * hidden :], 1, 0)
            sig = jax.nn.sigmoid(gate)
            gate_grad = (hid_grad * up * sig * (1.0 + gate * (1.0 - sig))).astype(LOW)
            up_grad = (hid_grad * gate * sig).astype(LOW)
            pair = jnp.concatenate([gate_grad, up_grad], 1)
            normed_grad = dot(pair, ffn_w[:, : 2 * hidden], 1, 1)
            ffn_grad = jnp.concatenate(
                [dot(normed_mid, pair, 0, 0).astype(LOW), dot(upstream_full, hid, 0, 0).astype(LOW)],
                1,
            )
            ffn_out = scatter_rows(place, ffn_grad)
            middle, middle_full, ffn_gain_grad = norm_back(
                normed_grad, full_mid, scale_mid, ffn_gains[layer], upstream, upstream_full
            )
            flat_grad = dot(middle_full, attn_w[:, 3 * width :], 1, 0).astype(LOW)
            out_grad = flat_grad.reshape(half_slots, block, width)
            query_grad, key_grad, value_grad, bias_grads[layer] = attend_back(
                queries, keys, values, same_kind, key_valid, biases[layer], logs, out_grad
            )
            key_value = scatter_keys(place, jnp.concatenate([key_grad, value_grad], -1))
            three = jnp.concatenate(
                [
                    rotate(query_grad, cosine, -sine),
                    rotate(key_value[:, :, :width], cosine, -sine),
                    key_value[:, :, width:],
                ],
                -1,
            )
            three = three.astype(LOW).reshape(tokens, 3 * width)
            normed_grad = dot(three, attn_w[:, : 3 * width], 1, 1)
            attn_grad = jnp.concatenate(
                [
                    dot(normed, three, 0, 0).astype(LOW),
                    dot(middle_full, attended.reshape(tokens, width), 0, 0).astype(LOW),
                ],
                1,
            )
            attn_out = scatter_rows(place, attn_grad)
            upstream, upstream_full, attn_gain_grad = norm_back(
                normed_grad, full, scale, attn_gains[layer], middle, middle_full
            )
            weight_grads[layer] = (
                attn_out[:, :width],
                attn_out[:, width : 2 * width],
                attn_out[:, 2 * width : 3 * width],
                attn_out[:, 3 * width :].T,
                ffn_out[:, :hidden],
                ffn_out[:, hidden : 2 * hidden],
                ffn_out[:, 2 * hidden :].T,
            )
            gain_grads[layer] = (attn_gain_grad, ffn_gain_grad)
        input_grad = place_tokens(place, upstream_full, positions, slots).astype(F32)

        mine = jnp.stack(
            [gain_grads[layer][i] for i in range(2) for layer in range(LAYERS)]
        )
        wide = lax.dynamic_update_slice_in_dim(
            jnp.zeros((2 * LAYERS, D), F32), mine, own_quarter * quarter, 1
        )
        wide = from_frame(place, wide)
        bias_wide = lax.dynamic_update_slice_in_dim(
            jnp.zeros((LAYERS, 4 * heads, 2), F32), jnp.stack(bias_grads), own_quarter * heads, 1
        )
        wide, bias_wide = lax.psum((wide, bias_wide), AXES)
        tensor = lax.axis_index("tensor")
        gains_out = lax.dynamic_slice_in_dim(wide, tensor * quarter, quarter, 1)
        bias_out = lax.dynamic_slice_in_dim(bias_wide, tensor * heads, heads, 1)
        stacks = [
            jnp.stack([weight_grads[layer][member] for layer in range(LAYERS)])
            for member in range(7)
        ]
        return (output, input_grad, *stacks, gains_out[:LAYERS], gains_out[LAYERS:], bias_out)

    return run


def solution(mesh):
    column = P(None, ("shard", "ctx"), "tensor")
    row = P(None, "tensor", ("shard", "ctx"))
    tokens = P("ctx", "shard", "tensor")
    gain = P(None, "tensor")
    bias = P(None, "tensor", None)
    return jax.shard_map(
        per_device(Place(mesh)),
        mesh=mesh,
        in_specs=(
            tokens, column, column, column, row, column, column, row,
            gain, gain, bias, P("shard"), P("ctx", "shard"), tokens,
        ),
        out_specs=(
            tokens, tokens, column, column, column, row, column, column, row, gain, gain, bias,
        ),
        check_vma=False,
    )
```

```python
import functools

import jax
import jax.numpy as jnp
from jax import lax
from jax.experimental import pallas as pl
from jax.experimental.pallas import tpu as pltpu
from jax.sharding import PartitionSpec as P

HD = 64
LAYERS = 2
epsilon = 1e-06
masked = -1e30
F32 = jnp.float32
LOW = jnp.bfloat16
AXES = ("shard", "o", "c", "zh", "zl")


def bits_of(count):
    width = count.bit_length() - 1
    assert 1 << width == count
    return width


def dot(left, right, left_dim, right_dim):
    return lax.dot_general(
        left, right, (((left_dim,), (right_dim,)), ((), ())), preferred_element_type=F32
    )


class Place:
    def __init__(self, mesh):
        self.n_shard = mesh.shape["shard"]
        self.n_o = mesh.shape["o"]
        self.n_ctx = 2 * self.n_o
        assert mesh.shape["zh"] == mesh.shape["zl"] == 2
        self.s_bits = bits_of(self.n_shard)
        self.o_bits = bits_of(self.n_o)
        self.dp = [("s", i) for i in reversed(range(self.s_bits))] + [
            ("o", i) for i in reversed(range(self.o_bits))
        ]

    def locate(self):
        self.zh = lax.axis_index("zh")
        self.zl = lax.axis_index("zl")
        self.s = lax.axis_index("shard")
        self.o = lax.axis_index("o")
        self.c = lax.axis_index("c")
        self.dp_bit = [((self.s if kind == "s" else self.o) >> i) & 1 for kind, i in self.dp]

    def away(self, bits):
        away_s = away_o = 0
        for bit, (kind, i) in zip(bits, self.dp):
            if kind == "s":
                away_s |= bit << i
            else:
                away_o |= bit << i
        return away_s, away_o

    def move(self, array, route):
        pairs = []
        for shard in range(self.n_shard):
            for ctx in range(self.n_ctx):
                for tensor in range(4):
                    s, o, c, zh, zl = route(shard, ctx // 2, ctx % 2, tensor // 2, tensor % 2)
                    source = (shard * self.n_ctx + ctx) * 4 + tensor
                    target = (s * self.n_ctx + 2 * o + c) * 4 + 2 * zh + zl
                    pairs.append((source, target))
        return lax.ppermute(array, AXES, pairs)

    def swap_core(self, array):
        return self.move(array, lambda s, o, c, zh, zl: (s, o, 1 - c, zh, zl))

    def swap_zl(self, array):
        return self.move(array, lambda s, o, c, zh, zl: (s, o, c, zh, 1 - zl))

    def swap_zh(self, array):
        return self.move(array, lambda s, o, c, zh, zl: (s, o, c, 1 - zh, zl))

    def swap_dp(self, array, index):
        kind, i = self.dp[index]
        if kind == "s":
            return self.move(array, lambda s, o, c, zh, zl: (s ^ (1 << i), o, c, zh, zl))
        return self.move(array, lambda s, o, c, zh, zl: (s, o ^ (1 << i), c, zh, zl))

    def near(self, array):
        return self.move(array, lambda s, o, c, zh, zl: (s, o, zh, c, zl))

    def far(self, array):
        return self.move(array, lambda s, o, c, zh, zl: (s, o, zh, 1 - c, zl))

    def far_back(self, array):
        return self.move(array, lambda s, o, c, zh, zl: (s, o, 1 - zh, c, zl))


def flip_if(bit, array, axis):
    return jnp.where(bit == 1, jnp.flip(array, axis), array)


def pick(flag, one, two):
    return jnp.where(flag == 1, one, two)


VMEM = pl.BlockSpec(memory_space=pltpu.VMEM)
SMEM = pl.BlockSpec(memory_space=pltpu.SMEM)
HBM = pl.BlockSpec(memory_space=pl.ANY)
MIB = 1024 * 1024
WORK = {
    "frame": 2,
    "qkv": 5,
    "attend": 8,
    "ffn": 9,
    "ffn_back": 10,
    "ffn_weights": 9,
    "attend_back_far": 9,
    "attend_back_near": 6,
    "qkv_back": 5,
    "attn_weights": 4,
    "leave": 3,
}


def shape(dims, kind):
    return jax.ShapeDtypeStruct(dims, kind)


def launch(body, outs, operands, specs, scratch=(), name=None):
    return pl.pallas_call(
        body,
        out_shape=outs,
        in_specs=specs,
        out_specs=[VMEM] * len(outs),
        scratch_shapes=list(scratch),
        compiler_params=pltpu.CompilerParams(vmem_limit_bytes=52 * MIB),
        cost_estimate=pl.CostEstimate(
            flops=int(WORK[name] * 1.15e9), bytes_accessed=1024, transcendentals=0
        ),
        name=name,
    )(*operands)


def load_rows(pieces, layout, spot, buffer, sems):
    copies = []
    for array, row, count, target, col in layout:
        source = pieces[array].at[pl.ds(pl.multiple_of(row(spot), count), count)]
        here = buffer.at[
            pl.ds(pl.multiple_of(target(spot), count), count),
            pl.ds(col, pieces[array].shape[1]),
        ]
        copies.append(pltpu.make_async_copy(source, here, sems.at[len(copies)]))
    for copy in copies:
        copy.start()
    return copies


def feature_start(spot, dc, dz, width):
    return pl.multiple_of((2 * (spot[0] ^ dc) + (spot[1] ^ dz)) * width, width)


def join_feats(spot, pieces, full):
    width = pieces[0].shape[1]
    for i, piece in enumerate(pieces):
        full[:, pl.ds(feature_start(spot, i // 2, i % 2, width), width)] = piece[...]


def each_rows(total, step, body):
    step = min(step, total)

    def one(i, carry):
        body(pl.ds(pl.multiple_of(i * step, step), step))
        return carry

    lax.fori_loop(0, total // step, one, 0)


def norm_rows(full, gain, normed, scale):
    def one(rows):
        x = full[rows, :].astype(F32)
        r = lax.rsqrt(jnp.mean(x * x, axis=1, keepdims=True) + epsilon)
        scale[rows, :] = r
        normed[rows, :] = (x * r * gain[...]).astype(LOW)

    each_rows(full.shape[0], 128, one)


def finish_back(spot, pieces, before_full, rows_full, scale, moved, full, own):
    width = moved.shape[1]
    depth = full.shape[1]
    join_feats(spot, pieces, full)
    start = feature_start(spot, 0, 0, width)

    def one(rows):
        u = full[rows, :].astype(F32)
        n = rows_full[rows, :].astype(F32) * scale[rows, :]
        dots = jnp.sum((u - before_full[rows, :].astype(F32)) * n, axis=1, keepdims=True)
        dots = dots * (1.0 / depth)
        full[rows, :] = (u - n * dots).astype(LOW)
        mine = rows_full[rows, pl.ds(start, width)].astype(F32) * scale[rows, :]
        own[rows, :] = moved[rows, :] - mine * dots

    each_rows(full.shape[0], 128, one)


def turn(values, cosine, sine):
    width = values.shape[1]
    lane = lax.broadcasted_iota(jnp.int32, values.shape, 1) % HD
    other = jnp.where(
        lane < HD // 2, pltpu.roll(values, width - HD // 2, 1), pltpu.roll(values, HD // 2, 1)
    )
    return values * cosine + other * sine


def store_parts(parts, spot, product, width):
    for i, part in enumerate(parts):
        part[...] = product(feature_start(spot, i // 2, i % 2, width)).astype(part.dtype)


def part_shapes(tokens, width):
    return [
        shape((tokens, width), F32),
        shape((tokens, width), F32),
        shape((tokens, width), LOW),
        shape((tokens, width), LOW),
    ]


def qkv_body(layout, joined, spot, *rest):
    pieces, rest = rest[: 1 if joined else 4], rest[1 if joined else 4 :]
    gain, cosine, sine = rest[:3]
    rest = rest[3:]
    count = 1 + max(entry[0] for entry in layout)
    weights = rest[:count]
    rest = rest[count:]
    if joined:
        full = pieces[0]
    else:
        full, rest = rest[0], rest[1:]
    normed, scale, queries, key_value, buffer, sems = rest
    copies = load_rows(weights, layout, spot, buffer, sems)
    if not joined:
        join_feats(spot, pieces, full)
    norm_rows(full, gain, normed, scale)
    for copy in copies:
        copy.wait()
    width = queries.shape[1]
    for i in range(3):
        product = dot(normed[...], buffer[:, i * width : (i + 1) * width], 1, 0)
        if i < 2:
            product = turn(product, cosine[...], sine[...])
        if i == 0:
            queries[...] = (product * 0.125).astype(LOW)
        else:
            key_value[:, (i - 1) * width : i * width] = product.astype(LOW)


def scores_of(q, k, same, row, step):
    return dot(q, k, 1, 1) + row + jnp.where(same, step, 0.0)


def attend_body(slots, n_blocks, layout, spot, bias, queries, own_kinds, kinds, masks, *rest):
    count = 1 + max(entry[0] for entry in layout)
    blocks = rest[:n_blocks]
    weights = rest[n_blocks : n_blocks + count]
    attended, logs, part0, part1, part2, part3, buffer, sems = rest[n_blocks + count :]
    copies = load_rows(weights, layout, spot, buffer, sems)
    tokens, width = queries.shape
    heads = width // HD
    size = tokens // slots
    wide = 2 * HD
    chunk = min(size, 256)
    side = lax.broadcasted_iota(jnp.int32, (1, wide), 1) // HD
    for slot in range(slots):
        keys = pl.ds(slot * size, size)
        for start in range(0, size, chunk):
            rows = pl.ds(slot * size + start, chunk)
            same = [
                own_kinds[rows, :] == kinds[slot : slot + 1, b * size : (b + 1) * size]
                for b in range(n_blocks)
            ]
            for pair in range(heads // 2):
                cols = slice(pair * wide, (pair + 1) * wide)
                values = slice(width + pair * wide, width + (pair + 1) * wide)
                both = queries[rows, cols]
                results = []
                for half in range(2):
                    head = 2 * pair + half
                    q = jnp.where(side == half, both, jnp.zeros_like(both))
                    step = bias[2 * head] - bias[2 * head + 1]
                    base = bias[2 * head + 1]
                    scores = [
                        scores_of(
                            q,
                            blocks[b][keys, cols],
                            same[b],
                            masks[slot : slot + 1, b * size : (b + 1) * size] + base,
                            step,
                        )
                        for b in range(n_blocks)
                    ]
                    highest = functools.reduce(
                        jnp.maximum, [jnp.max(s, axis=1, keepdims=True) for s in scores]
                    )
                    powers = [jnp.exp(s - highest) for s in scores]
                    total = functools.reduce(
                        lambda a, b: a + b, [jnp.sum(p, axis=1, keepdims=True) for p in powers]
                    )
                    product = functools.reduce(
                        lambda a, b: a + b,
                        [
                            dot(powers[b].astype(LOW), blocks[b][keys, values], 1, 0)
                            for b in range(n_blocks)
                        ],
                    )
                    results.append(product * (1.0 / total))
                    logs[rows, head : head + 1] = highest + jnp.log(total)
                attended[rows, cols] = jnp.where(side == 0, results[0], results[1]).astype(LOW)
    for copy in copies:
        copy.wait()
    share = part0.shape[1]
    last = slice(3 * width, 4 * width)
    store_parts(
        (part0, part1, part2, part3),
        spot,
        lambda start: dot(attended[...], buffer[pl.ds(start, share), last], 1, 1),
        share,
    )


def ffn_body(layout, spot, p0, p1, p2, p3, gain, *rest):
    count = 1 + max(entry[0] for entry in layout)
    weights = rest[:count]
    full, normed, scale, gate, up, hid, part0, part1, part2, part3, buffer, sems = rest[count:]
    copies = load_rows(weights, layout, spot, buffer, sems)
    join_feats(spot, (p0, p1, p2, p3), full)
    norm_rows(full, gain, normed, scale)
    for copy in copies:
        copy.wait()
    hidden = hid.shape[1]
    tile = 256

    def one(i, carry):
        start = pl.multiple_of(i * tile, tile)
        here = pl.ds(start, tile)
        g = dot(normed[...], buffer[:, here], 1, 0)
        u = dot(normed[...], buffer[:, pl.ds(pl.multiple_of(hidden + start, tile), tile)], 1, 0)
        gate[:, here] = g.astype(LOW)
        up[:, here] = u.astype(LOW)
        hid[:, here] = (g * jax.nn.sigmoid(g) * u).astype(LOW)
        return carry

    lax.fori_loop(0, hidden // tile, one, 0)
    share = part0.shape[1]
    store_parts(
        (part0, part1, part2, part3),
        spot,
        lambda start: dot(hid[...], buffer[pl.ds(start, share), 2 * hidden : 3 * hidden], 1, 1),
        share,
    )


def ffn_back_body(finish, layout, spot, *rest):
    count = 1 + max(entry[0] for entry in layout)
    if finish:
        p0, p1, p2, p3, before_full, rows_full, scale, moved = rest[:8]
        rest = rest[8:]
    else:
        full_in = rest[0]
        rest = rest[1:]
    gate, up = rest[:2]
    weights = rest[2 : 2 + count]
    rest = rest[2 + count :]
    if finish:
        full, own = rest[:2]
        rest = rest[2:]
    gate_grad, up_grad, part0, part1, part2, part3, buffer, sems = rest
    copies = load_rows(weights, layout, spot, buffer, sems)
    if finish:
        finish_back(
            spot, (p0, p1, p2, p3), before_full, rows_full, scale, moved, full, own
        )
    else:
        full = full_in
    for copy in copies:
        copy.wait()
    hidden = gate.shape[1]
    tile = 256

    def one(i, carry):
        start = pl.multiple_of(i * tile, tile)
        here = pl.ds(start, tile)
        grad = dot(
            full[...], buffer[:, pl.ds(pl.multiple_of(2 * hidden + start, tile), tile)], 1, 0
        )
        g = gate[:, here].astype(F32)
        sig = jax.nn.sigmoid(g)
        gate_grad[:, here] = (
            grad * up[:, here].astype(F32) * sig * (1.0 + g * (1.0 - sig))
        ).astype(LOW)
        up_grad[:, here] = (grad * g * sig).astype(LOW)
        return carry

    lax.fori_loop(0, hidden // tile, one, 0)
    share = part0.shape[1]
    store_parts(
        (part0, part1, part2, part3),
        spot,
        lambda start: dot(gate_grad[...], buffer[pl.ds(start, share), :hidden], 1, 1)
        + dot(up_grad[...], buffer[pl.ds(start, share), hidden : 2 * hidden], 1, 1),
        share,
    )


def grad_columns(pairs, blocks, operands, rows, out, out_rows):
    col = 0
    for left, right in pairs:
        right = operands[right]
        width = right.shape[1]
        for start in range(0, width, 512):
            tile = min(512, width - start)
            out[out_rows, col : col + tile] = dot(
                blocks[left][:, rows], right[:, start : start + tile], 0, 0
            ).astype(LOW)
            col += tile


def arrange(operands, pairs, spot, order, scratch):
    blocks = {}
    for buffer, left in zip(scratch, sorted({left for left, _ in pairs})):
        width = buffer.shape[1] // len(order)
        for i, block in enumerate(order):
            at = pl.multiple_of(block(spot) * width, width)
            buffer[:, i * width : (i + 1) * width] = operands[left][:, pl.ds(at, width)]
        blocks[left] = buffer
    return blocks


def weight_grad_group_body(pairs, order, fit, spot, *refs):
    operands, (out,) = refs[: len(refs) - 1 - fit], refs[len(refs) - 1 - fit :][:1]
    blocks = arrange(operands, pairs, spot, order, refs[len(refs) - fit :]) if fit else operands
    step = min(256, out.shape[0])
    for start in range(0, out.shape[0], step):
        rows = slice(start, start + step)
        grad_columns(pairs, blocks, operands, rows, out, rows)


def relative_order(k):
    def bits(i):
        return [(i >> (k - 1 - j)) & 1 for j in range(k)]

    first = [(tuple(bits(i)), 0) for i in range(2**k)]
    second = [(tuple(reversed(bits(i))), 1) for i in range(2**k)]
    return first + second


def weight_grad_sent_body(pairs, order, fit, spot, *refs):
    operands, outs = refs[: len(refs) - 4 - fit], refs[len(refs) - 4 - fit :][:4]
    blocks = arrange(operands, pairs, spot, order, refs[len(refs) - fit :]) if fit else operands
    depth = outs[0].shape[0]
    for i, out in zip((1, 3, 0, 2), outs):
        rows = slice(i * depth, (i + 1) * depth)
        grad_columns(pairs, blocks, operands, rows, out, slice(0, depth))


def attend_back_body(
    slots, n_blocks, first_block, first, layout, spot, bias, queries, attended, logs, *rest
):
    count = 1 + max([entry[0] for entry in layout] + [-1])
    own_kinds, kinds, masks = rest[:3]
    blocks = rest[3 : 3 + n_blocks]
    rest = rest[3 + n_blocks :]
    tokens, width = queries.shape
    if first:
        p0, p1, p2, p3, before_full, rows_full, scale, moved = rest[:8]
        weights = rest[8 : 8 + count]
        full, own, out_grad, deltas, query_grad, same_sum = rest[8 + count : 14 + count]
        grads = rest[14 + count : 14 + count + n_blocks]
        buffer, sems = rest[14 + count + n_blocks :]
        copies = load_rows(weights, layout, spot, buffer, sems)
        finish_back(
            spot, (p0, p1, p2, p3), before_full, rows_full, scale, moved, full, own
        )
        for copy in copies:
            copy.wait()
        out_grad[...] = dot(full[...], buffer[:, 3 * width :], 1, 0).astype(LOW)
    else:
        out_grad, deltas, query_before = rest[:3]
        query_grad, same_sum = rest[3:5]
        grads = rest[5 : 5 + n_blocks]
    heads = width // HD
    size = tokens // slots
    wide = 2 * HD
    side = lax.broadcasted_iota(jnp.int32, (1, wide), 1) // HD
    if first:
        for head in range(heads):
            cols = slice(head // 2 * wide, (head // 2 + 1) * wide)
            product = attended[:, cols].astype(F32) * out_grad[:, cols].astype(F32)
            deltas[:, head : head + 1] = jnp.sum(
                jnp.where(side == head % 2, product, 0.0), axis=1, keepdims=True
            )
    same_sum[...] = jnp.zeros_like(same_sum)
    for slot in range(slots):
        keys = pl.ds(slot * size, size)
        for pair in range(heads // 2):
            cols = slice(pair * wide, (pair + 1) * wide)
            values = slice(width + pair * wide, width + (pair + 1) * wide)
            both = queries[keys, cols]
            grad_both = out_grad[keys, cols]
            query_total = None
            for b in range(n_blocks):
                place_b = first_block + b
                these = slice(place_b * size, (place_b + 1) * size)
                same = own_kinds[keys, :] == kinds[slot : slot + 1, these]
                k = blocks[b][keys, cols]
                v = blocks[b][keys, values]
                key_total = value_total = None
                for half in range(2):
                    head = 2 * pair + half
                    q = jnp.where(side == half, both, jnp.zeros_like(both))
                    g = jnp.where(side == half, grad_both, jnp.zeros_like(both))
                    step = bias[2 * head] - bias[2 * head + 1]
                    base = bias[2 * head + 1]
                    scores = scores_of(q, k, same, masks[slot : slot + 1, these] + base, step)
                    soft = jnp.exp(scores - logs[keys, head : head + 1])
                    soft_grad = dot(g, v, 1, 1)
                    score_grad = soft * (soft_grad - deltas[keys, head : head + 1])
                    same_sum[head : head + 1, :] += jnp.sum(
                        jnp.where(same, score_grad, 0.0), axis=0, keepdims=True
                    )
                    low = score_grad.astype(LOW)
                    masked_k = jnp.where(side == half, k, jnp.zeros_like(k))
                    query_part = dot(low, masked_k, 1, 0)
                    key_part = dot(low, q, 0, 0)
                    value_part = dot(soft.astype(LOW), g, 0, 0)
                    query_total = query_part if query_total is None else query_total + query_part
                    key_total = key_part if key_total is None else key_total + key_part
                    value_total = value_part if value_total is None else value_total + value_part
                grads[b][keys, cols] = key_total.astype(grads[b].dtype)
                grads[b][keys, values] = value_total.astype(grads[b].dtype)
            query_total = query_total * 0.125
            if not first:
                query_total = query_total + query_before[keys, cols]
            query_grad[keys, cols] = query_total


def qkv_back_body(layout, n_received, spot, query_grad, key_value, cosine, sine, *rest):
    count = 1 + max(entry[0] for entry in layout)
    received = rest[:n_received]
    weights = rest[n_received : n_received + count]
    three, part0, part1, part2, part3, buffer, sems = rest[n_received + count :]
    copies = load_rows(weights, layout, spot, buffer, sems)
    width = query_grad.shape[1]
    total = key_value[...]
    for other in received:
        total = total + other[...].astype(F32)
    three[:, :width] = turn(query_grad[...], cosine[...], -sine[...]).astype(LOW)
    three[:, width : 2 * width] = turn(total[:, :width], cosine[...], -sine[...]).astype(LOW)
    three[:, 2 * width :] = total[:, width:].astype(LOW)
    for copy in copies:
        copy.wait()
    share = part0.shape[1]
    store_parts(
        (part0, part1, part2, part3),
        spot,
        lambda start: dot(three[...], buffer[pl.ds(start, share), : 3 * width], 1, 1),
        share,
    )


def frame_body(slots, masked_rows, table, spot, mine, other, *rest):
    valid, full = (rest[0], rest[1]) if masked_rows else (None, rest[0])
    positions = mine.shape[2]
    blocks = table.shape[0]
    lanes = full.shape[1] // blocks
    for near in range(2):
        source = mine if near == 0 else other
        for slot in range(slots):
            start = pl.multiple_of((2 * slot + (spot[0] ^ near)) * positions, positions)
            for spot_out in range(blocks):
                block = table[spot_out]
                per = blocks // 4
                quarter = block // per
                which = (2 * ((quarter // 2) ^ spot[2])) + ((quarter % 2) ^ spot[1])
                lane = pl.multiple_of((block % per) * lanes, lanes)
                values = source[which, slot, :, pl.ds(lane, lanes)]
                if masked_rows:
                    values = values * valid[pl.ds(start, positions), :].astype(LOW)
                full[pl.ds(start, positions), spot_out * lanes : (spot_out + 1) * lanes] = values


def unframe(slots, table, spot, full, keep, send):
    positions = keep.shape[1]
    blocks = table.shape[0]
    lanes = full.shape[1] // blocks
    per = blocks // 4
    for away, out in ((0, keep), (1, send)):
        quarter = 2 * (spot[2] ^ away) + spot[1]
        for slot in range(slots):
            start = pl.multiple_of((2 * slot + spot[0]) * positions, positions)
            for i in range(per):
                at = table[quarter * per + i]
                lane = pl.multiple_of(at * lanes, lanes)
                out[slot, :, i * lanes : (i + 1) * lanes] = full[
                    pl.ds(start, positions), pl.ds(lane, lanes)
                ]


def leave_body(slots, finish, fit, spot, table, *rest):
    pieces, rest = rest[:4], rest[4:]
    if finish:
        before_full, rows_full, scale, moved = rest[:4]
        outs, full, own = rest[4:-2], rest[-2], rest[-1]
        finish_back(spot, pieces, before_full, rows_full, scale, moved, full, own)
    else:
        outs, full = rest[:-1], rest[-1]
        join_feats(spot, pieces, full)
    if fit:
        unframe(slots, table, spot, full, *outs)
    else:
        outs[0][...] = full[...]


def after(value, *others):
    return lax.optimization_barrier((value, others))[0]


def take_rows(place, natural, other):
    same = (place.c == place.zh).astype(jnp.int32)
    kept = pick(same, natural, other)
    received = place.swap_core(pick(same, other, natural))
    return pick(same, kept, received), pick(same, received, kept)


def return_rows(place, first, second):
    same = (place.c == place.zh).astype(jnp.int32)
    kept = pick(same, first, second)
    received = place.swap_core(pick(same, second, first))
    return pick(same, kept, received), pick(same, received, kept)


def gather_rows_swap(place, both, waits=()):
    k = len(place.dp)
    pieces, layout, early = [], [], []
    count = both[0].shape[0]
    for side, order in ((0, list(range(k))), (1, list(reversed(range(k))))):
        held, blocks = [both[side]], [(0,) * k]
        for index in order:
            send = held[0] if len(held) == 1 else jnp.concatenate(after(held, *waits), 0)
            held.append(place.swap_dp(send, index))
            if len(held) == 2:
                early.append(held[1])
            blocks += [b[:index] + (1 - b[index],) + b[index + 1 :] for b in blocks]
        at = 0
        for piece in held:
            for row in range(0, piece.shape[0], count):
                target = row_block(place, blocks[at], side)
                layout.append(
                    (
                        len(pieces),
                        lambda spot, row=row: row,
                        count,
                        lambda spot, target=target: target(spot) * count,
                        0,
                    )
                )
                at += 1
            pieces.append(piece)
    return pieces, layout, early


def row_block(place, bits, side):
    away_s, away_o = place.away(bits)
    chips = place.n_o
    return lambda spot: (
        ((spot[3] ^ away_s) * chips + (spot[4] ^ away_o)) * 2 + (spot[2] ^ side)
    )


def gather_rows_group(place, chunks):
    both = jnp.concatenate(
        [jnp.concatenate([chunk[side] for chunk in chunks], 1) for side in range(2)], 0
    )
    rows = lax.all_gather(both, ("shard", "o"), axis=0, tiled=True)
    chips = place.n_shard * place.n_o
    count = rows.shape[0] // (2 * chips)
    layout = [
        (
            0,
            lambda spot, i=i: i * count,
            count,
            lambda spot, i=i: (i - i % 2 + (i % 2 ^ spot[2])) * count,
            0,
        )
        for i in range(2 * chips)
    ]
    return [rows], layout


def join_chunks(*chunks):
    arrays, layout, column = [], [], 0
    for pieces, lay in chunks:
        layout += [(a + len(arrays), row, count, target, column) for a, row, count, target, _ in lay]
        arrays = arrays + pieces
        column += pieces[0].shape[1]
    return arrays, layout


def scatter_rows_group(place, partial):
    rows = lax.psum_scatter(partial, ("shard", "o"), scatter_dimension=0, tiled=True)
    half = rows.shape[0] // 2
    return rows[:half], rows[half:]


def scatter_start(place, sent, other_sent):
    return place.swap_dp(sent, 0), place.swap_dp(other_sent, len(place.dp) - 1)


def scatter_rest(place, received, kept, waits=()):
    k = len(place.dp)
    ends = []
    for got, keep, order in (
        (received[0], kept[0], list(range(k))),
        (received[1], kept[1], list(reversed(range(k)))),
    ):
        part = (keep.astype(F32) + got.astype(F32)).astype(LOW)
        for index in order[1:]:
            middle = part.shape[0] // 2
            got = place.swap_dp(after(part[middle:], *waits), index)
            part = (part[:middle].astype(F32) + got.astype(F32)).astype(LOW)
        ends.append(part)
    return ends


def gather_feats(place, share):
    other = place.swap_zl(share)
    return [share, other, place.swap_core(share), place.swap_core(other)]


def scatter_feats(place, parts, beside=None):
    kept, kept_pair, sent, sent_pair = parts
    middle = (kept_pair + place.swap_core(sent_pair).astype(F32)).astype(LOW)
    near = kept + place.swap_core(sent).astype(F32)
    received = place.swap_zl(middle)
    done = None if beside is None else beside(middle)
    return near + after(received, done).astype(F32), done


def gather_keys(place, own):
    pieces = [own]
    for index in reversed(range(place.s_bits, len(place.dp))):
        pieces = pieces + [place.swap_dp(piece, index) for piece in pieces]
    return pieces


def per_device(place):
    def run(
        inputs,
        w_query,
        w_key,
        w_value,
        w_out,
        w_gate,
        w_up,
        w_down,
        attn_gain,
        ffn_gain,
        variate_bias,
        lengths,
        variates,
        cotangent,
    ):
        place.locate()
        positions, slots, quarter = inputs.shape
        depth = quarter * 4
        half_slots = slots // 2
        block = 2 * positions
        n_o = place.n_ctx // 2
        tokens = half_slots * block
        width = w_query.shape[2]
        heads = width // HD
        hidden = w_gate.shape[2]
        own_quarter = 2 * place.c + place.zl
        spot = jnp.stack([place.c, place.zl, place.zh, place.s, place.o]).astype(jnp.int32)
        k = len(place.dp)
        n_blocks = 2 ** (k + 1)
        block_rows = depth // n_blocks
        table = jnp.arange(n_blocks, dtype=jnp.int32)
        block_rows = depth // n_blocks
        lanes_fit = block_rows % 128 == 0

        attn_packs = [
            jnp.concatenate([w_query[i], w_key[i], w_value[i], w_out[i].T], 1)
            for i in range(LAYERS)
        ]

        def swap_slots(natural):
            first, second = natural[:, :half_slots], natural[:, half_slots:]
            return place.swap_zh(pick(place.zh, first, second).transpose(1, 0, 2))

        def token_quarters(natural, received):
            first, second = natural[:, :half_slots], natural[:, half_slots:]
            own = pick(place.zh, second, first).transpose(1, 0, 2)
            two = jnp.stack([own, received])
            other = place.swap_zl(two)
            mine = jnp.stack([two, other], 1).reshape(4, half_slots, positions, quarter)
            return mine, place.swap_core(mine), other

        def token_rows(quarters, valid):
            mine, other = quarters[:2]
            if lanes_fit:
                operands = [table, spot, mine, other] + ([] if valid is None else [valid])
                return launch(
                    functools.partial(frame_body, half_slots, valid is not None),
                    [shape((tokens, depth), LOW)],
                    operands,
                    [SMEM, SMEM] + [VMEM] * (len(operands) - 2),
                    name="frame",
                )[0]
            by_core = jnp.stack([pick(place.c, other, mine), pick(place.c, mine, other)], 0)
            cut = by_core.reshape(2, 2, 2, half_slots, positions, quarter)
            cut = flip_if(place.zl, flip_if(place.zh, cut, 1), 2)
            rows = cut.transpose(3, 0, 4, 1, 2, 5).reshape(tokens, depth)
            return rows if valid is None else rows * valid.astype(LOW)

        def natural_rows(pieces, pending=()):
            outs = [shape((half_slots, positions, quarter), LOW)] * 2
            scratch = [pltpu.VMEM((tokens, depth), LOW)]
            if pending:
                scratch.append(pltpu.VMEM((tokens, quarter), F32))
            outs = launch(
                functools.partial(leave_body, half_slots, bool(pending), lanes_fit),
                outs if lanes_fit else [shape((tokens, depth), LOW)],
                [spot, table, *pieces, *pending],
                [SMEM] * 2 + [VMEM] * (4 + len(pending)),
                scratch,
                name="leave",
            )
            if lanes_fit:
                keep, send = outs
            else:
                cut = outs[0].reshape(
                    half_slots, 2, positions, 2, 2, quarter
                )
                cut = pick(place.c, cut[:, 1], cut[:, 0])
                cut = pick(place.zl, cut[:, :, :, 1], cut[:, :, :, 0])
                keep = pick(place.zh, cut[:, :, 1], cut[:, :, 0])
                send = pick(place.zh, cut[:, :, 0], cut[:, :, 1])
            received = place.swap_zh(send)
            both = jnp.concatenate(
                [pick(place.zh, received, keep), pick(place.zh, keep, received)], 0
            )
            return both.transpose(1, 0, 2)

        zh_done = swap_slots(inputs)
        mine, other, zl_done = token_quarters(inputs, zh_done)
        small = jnp.concatenate(
            [attn_gain.reshape(-1), ffn_gain.reshape(-1), variate_bias.reshape(-1)]
        ).reshape(1, -1)
        small = after(small, zh_done)
        pair = jnp.stack([small, place.swap_zh(small)], 0)
        all_small = jnp.stack([pair, place.swap_zl(pair)], 2)
        all_small = flip_if(place.zl, flip_if(place.zh, all_small, 0), 2)
        small = all_small.reshape(4, -1)
        cut = LAYERS * quarter
        natural_gains = jnp.concatenate(
            [
                small[:, i * cut : (i + 1) * cut]
                .reshape(4, LAYERS, quarter)
                .transpose(1, 0, 2)
                .reshape(LAYERS, depth)
                for i in range(2)
            ]
        )
        gains = natural_gains
        biases = lax.dynamic_index_in_dim(
            small[:, 2 * cut :].reshape(4, LAYERS, 2 * heads), own_quarter, 0, keepdims=False
        )

        ffn_chunks = [(w_gate[i], w_up[i], w_down[i].T) for i in range(LAYERS)]

        def take_late(natural, start, use):
            natural = after(natural, start)
            return take_rows(place, natural, after(place.swap_zh(natural), use))

        attn_both = take_late(attn_packs[0], zh_done, zh_done)
        gate = after(ffn_chunks[0][0], attn_both)
        gate_other = place.swap_zh(gate)
        *first_attn, early = gather_rows_swap(place, attn_both)
        up = after(ffn_chunks[0][1], early)
        up_other = place.swap_zh(up)

        own_kinds = after(variates.astype(F32), zl_done)
        rest = place.swap_core(own_kinds)
        own_kinds = jnp.concatenate(
            [pick(place.c, rest, own_kinds), pick(place.c, own_kinds, rest)], 0
        )
        own_kinds = pick(place.zh, own_kinds[:, half_slots:], own_kinds[:, :half_slots]).T
        kinds = jnp.concatenate(gather_keys(place, own_kinds), 1)
        own_kinds = own_kinds.reshape(tokens, 1)
        own_lengths = pick(place.zh, lengths[half_slots:], lengths[:half_slots])
        own_positions = place.o * block + jnp.arange(block, dtype=jnp.int32)
        chips = jnp.arange(n_o, dtype=jnp.int32) ^ place.o
        key_positions = (
            chips[:, None] * block + jnp.arange(block, dtype=jnp.int32)[None, :]
        ).reshape(-1)
        masks = jnp.where(key_positions[None, :] < own_lengths[:, None], 0.0, masked).astype(F32)
        valid = (own_positions[None, :] < own_lengths[:, None]).astype(F32).reshape(tokens, 1)
        index = jnp.arange(width, dtype=jnp.int32) % HD
        inverse = 10000.0 ** (-(2.0 * (index % (HD // 2)).astype(F32)) / HD)
        angles = own_positions.astype(F32)[:, None] * inverse[None, :]
        cosine = jnp.tile(jnp.cos(angles), (half_slots, 1))
        sine = jnp.tile(
            jnp.where(index < HD // 2, -1.0, 1.0)[None, :] * jnp.sin(angles), (half_slots, 1)
        )

        def share_of(rows):
            return lax.dynamic_slice_in_dim(rows, own_quarter * quarter, quarter, -1)

        attn_buffer = [
            pltpu.VMEM((depth, 4 * width), LOW),
            pltpu.SemaphoreType.DMA((n_blocks,)),
        ]
        ffn_buffer = [
            pltpu.VMEM((depth, 3 * hidden), LOW),
            pltpu.SemaphoreType.DMA((2 * n_blocks,)),
        ]
        rows_low = shape((tokens, depth), LOW)
        column = shape((tokens, 1), F32)
        share_f32 = shape((tokens, quarter), F32)
        parts = part_shapes(tokens, quarter)

        if lanes_fit:
            full = launch(
                functools.partial(frame_body, half_slots, False),
                [rows_low],
                [table, spot, mine, other],
                [SMEM, SMEM, VMEM, VMEM],
                name="frame",
            )[0]
        else:
            by_core = jnp.stack([pick(place.c, other, mine), pick(place.c, mine, other)], 0)
            cut4 = by_core.reshape(2, 2, 2, half_slots, positions, quarter)
            cut4 = flip_if(place.zl, flip_if(place.zh, cut4, 1), 2)
            full = cut4.transpose(3, 0, 4, 1, 2, 5).reshape(tokens, depth)

        pieces = [full]
        current = share_of(full).astype(F32)
        kept, weights = [], []
        attn_w, attn_lay = first_attn
        nothing = ()
        for layer in range(LAYERS):
            first, more = layer == 0, layer + 1 < LAYERS
            outs = launch(
                functools.partial(qkv_body, attn_lay, layer == 0),
                ([] if layer == 0 else [rows_low])
                + [
                    rows_low,
                    column,
                    shape((tokens, width), LOW),
                    shape((tokens, 2 * width), LOW),
                ],
                [spot, *pieces, gains[layer : layer + 1], cosine, sine, *attn_w],
                [SMEM] + [VMEM] * (3 + len(pieces)) + [HBM] * len(attn_w),
                attn_buffer,
                name="qkv",
            )
            if layer > 0:
                full, outs = outs[0], outs[1:]
            normed, scale, queries, key_value = outs
            blocks = gather_keys(place, key_value)
            if first:
                gate_both = take_rows(place, gate, after(gate_other, key_value))
                up_both = take_rows(place, up, after(up_other, key_value))
                down = after(ffn_chunks[0][2], key_value)
                down_other = place.swap_zh(down)
                blocks = after(blocks, down_other, gate_both, up_both)
                gate_up = gather_rows_group(place, after((gate_both, up_both), blocks))
            if layer == LAYERS - 1:
                late_cotangent = after(cotangent, key_value)
                cotangent_quarters = token_quarters(late_cotangent, swap_slots(late_cotangent))
                upstream_full = token_rows(cotangent_quarters, valid)
                blocks = after(blocks, upstream_full)
            if more:
                attn_next = after(attn_packs[layer + 1], blocks)
                attn_other = place.swap_zh(attn_next)
            attended, logs, *sums = launch(
                functools.partial(attend_body, half_slots, n_o, attn_lay),
                [shape((tokens, width), LOW), shape((tokens, heads), F32), *parts],
                [spot, biases[layer], queries, own_kinds, kinds, masks, *blocks, *attn_w],
                [SMEM] * 2 + [VMEM] * (4 + n_o) + [HBM] * len(attn_w),
                attn_buffer,
                name="attend",
            )
            if more:
                sums = after(sums, attn_other)
                chunks = ffn_chunks[layer + 1]
                others = [place.swap_zh(after(chunks[0], sums))]
            if first:
                down_both = take_rows(place, down, after(down_other, attended))

            def reduce_side(sent):
                return list(others) if more else []

            shared, _ = scatter_feats(place, sums, reduce_side)
            middle = current + shared
            if first:
                down_w, down_lay, early = gather_rows_swap(place, down_both, (middle,))
            mid_pieces = gather_feats(place, middle.astype(LOW))
            if more:
                others.append(place.swap_zh(after(chunks[1], middle)))
                attn_both = take_rows(place, attn_next, after(attn_other, middle))
                mid_pieces = after(mid_pieces, others[1], attn_both)
            if first:
                mid_pieces = after(mid_pieces, down_w)
                ffn_w, ffn_lay = join_chunks(gate_up, (down_w, down_lay))
            if more:
                others.append(place.swap_zh(after(chunks[2], mid_pieces)))
                next_w, next_lay, early = gather_rows_swap(
                    place, after(attn_both, mid_pieces, ffn_w), nothing
                )
            full_mid, normed_mid, scale_mid, gate, up, hid, *sums = launch(
                functools.partial(ffn_body, ffn_lay),
                [
                    rows_low,
                    rows_low,
                    column,
                    *[shape((tokens, hidden), LOW)] * 3,
                    *parts,
                ],
                [
                    spot,
                    *mid_pieces,
                    gains[LAYERS + layer : LAYERS + layer + 1],
                    *ffn_w,
                ],
                [SMEM] + [VMEM] * 5 + [HBM] * len(ffn_w),
                ffn_buffer,
                name="ffn",
            )
            weights.append((attn_w, attn_lay, ffn_w, ffn_lay))
            if more:
                sums = after(sums, early)

            def take_side(sent):
                return [
                    take_rows(place, chunk, after(other, sent))
                    for chunk, other in zip(chunks, others)
                ]

            shared, ffn_both = scatter_feats(place, sums, take_side if more else None)
            if more:
                attn_w, attn_lay = next_w, next_lay
                ffn_w, ffn_lay = gather_rows_group(place, ffn_both)
            current = middle + shared
            kept.append(
                (
                    full,
                    normed,
                    scale,
                    queries,
                    blocks,
                    attended,
                    logs,
                    full_mid,
                    normed_mid,
                    scale_mid,
                    gate,
                    up,
                    hid,
                )
            )
            pieces = gather_feats(place, current.astype(LOW))

        last = pieces
        natural_valid = (
            ((2 * place.o + place.c) * positions + jnp.arange(positions, dtype=jnp.int32))[:, None]
            < lengths[None, :]
        )

        upstream = share_of(upstream_full).astype(F32)

        def step_back(sums, full_rows, row_scale, gain, before, beside):
            shared, done = scatter_feats(place, sums, beside)
            own_rows = share_of(full_rows).astype(F32) * row_scale
            gain_grad = jnp.sum(shared * own_rows, 0)
            moved = before + row_scale * (shared * share_of(gain)[None, :])
            return moved, gather_feats(place, moved.astype(LOW)), gain_grad, done

        sent_order = [row_block(place, bits, side) for bits, side in relative_order(k)]
        group_order = [
            lambda spot, i=i: i - i % 2 + (i % 2 ^ spot[2]) for i in range(n_blocks)
        ]

        def weight_grads_of(swapped, pairs, operands, columns, name, ready):
            operands = after(operands, ready)
            lefts = sorted({left for left, _ in pairs})
            order = sent_order if swapped else group_order
            scratch = []
            if lanes_fit:
                scratch = [pltpu.VMEM((tokens, depth), LOW) for _ in lefts]
            else:
                index = jnp.stack([block(spot) for block in order])
                operands = [
                    jnp.take(array.reshape(tokens, n_blocks, block_rows), index, axis=1).reshape(
                        tokens, depth
                    )
                    if i in lefts
                    else array
                    for i, array in enumerate(operands)
                ]
            return launch(
                functools.partial(
                    weight_grad_sent_body if swapped else weight_grad_group_body,
                    pairs,
                    order,
                    len(scratch),
                ),
                [shape((depth // 4, columns), LOW)] * 4
                if swapped
                else [shape((depth, columns), LOW)],
                [spot, *operands],
                [SMEM] + [VMEM] * len(operands),
                scratch,
                name=name,
            )

        weight_grads = [None] * LAYERS

        def keep_grads(layer, ffn_out, attn_out):
            attn_out, ffn_out = attn_out.astype(F32), ffn_out.astype(F32)
            weight_grads[layer] = (
                attn_out[:, :width],
                attn_out[:, width : 2 * width],
                attn_out[:, 2 * width : 3 * width],
                attn_out[:, 3 * width :].T,
                ffn_out[:, :hidden],
                ffn_out[:, hidden : 2 * hidden],
                ffn_out[:, 2 * hidden :].T,
            )

        late = None
        gain_grads = [None] * LAYERS
        bias_grads = [None] * LAYERS
        half_keys = max(n_o // 2, 1)
        pending = None
        for layer in reversed(range(LAYERS)):
            attn_w, attn_lay, ffn_w, ffn_lay = weights[layer]
            (
                full,
                normed,
                scale,
                queries,
                blocks,
                attended,
                logs,
                full_mid,
                normed_mid,
                scale_mid,
                gate,
                up,
                hid,
            ) = kept[layer]
            hidden_low = shape((tokens, hidden), LOW)
            if pending is None:
                gate_grad, up_grad, *sums = launch(
                    functools.partial(ffn_back_body, False, ffn_lay),
                    [hidden_low, hidden_low, *parts],
                    [spot, upstream_full, gate, up, *ffn_w],
                    [SMEM] + [VMEM] * 3 + [HBM] * len(ffn_w),
                    ffn_buffer,
                    name="ffn_back",
                )
            else:
                upstream_full, upstream, gate_grad, up_grad, *sums = launch(
                    functools.partial(ffn_back_body, True, ffn_lay),
                    [rows_low, share_f32, hidden_low, hidden_low, *parts],
                    [spot, *pending, gate, up, *ffn_w],
                    [SMEM] + [VMEM] * 10 + [HBM] * len(ffn_w),
                    ffn_buffer,
                    name="ffn_back",
                )
            if layer == LAYERS - 1:
                output = natural_rows(last)
                sums = after(sums, output)
                output = output * natural_valid[:, :, None].astype(LOW)
            if late is not None:
                late_ffn, late_got, late_kept = late
                sums = after(sums, late_got)
            ffn_grads = functools.partial(
                weight_grads_of,
                False,
                ((0, 1), (0, 2), (3, 4)),
                [normed_mid, gate_grad, up_grad, upstream_full, hid],
                3 * hidden,
                "ffn_weights",
            )

            def ffn_side(sent):
                partial = ffn_grads(sent)
                if late is None:
                    return partial, None
                ends = scatter_rest(place, after(late_got, sent), late_kept)
                return after(partial, ends), ends

            moved, pieces, ffn_gain_grad, (ffn_partial, late_ends) = step_back(
                sums, full_mid, scale_mid, gains[LAYERS + layer], upstream, ffn_side
            )
            ffn_rows = scatter_rows_group(place, *ffn_partial)
            if late is not None:
                own_ffn, other_ffn = return_rows(place, *after(late_ffn, moved))
                pieces = after(pieces, other_ffn)
                others = [
                    place.swap_zh(after(other_ffn[:, :hidden], pieces)),
                ]
            common = [queries, attended, logs, own_kinds, kinds, masks]
            later = blocks[half_keys:] if n_o > 1 else blocks
            early = blocks[:half_keys] if n_o > 1 else []
            start = half_keys if n_o > 1 else 0
            middle_full, middle, out_grad, deltas, query_grad, same_sum, *sent = launch(
                functools.partial(
                    attend_back_body, half_slots, len(later), start, True, attn_lay
                ),
                [
                    rows_low,
                    share_f32,
                    shape((tokens, width), LOW),
                    shape((tokens, heads), F32),
                    shape((tokens, width), F32),
                    shape((heads, block), F32),
                    *[shape((tokens, 2 * width), LOW)] * len(later),
                ],
                [
                    spot,
                    biases[layer],
                    *common,
                    *later,
                    *pieces,
                    upstream_full,
                    full_mid,
                    scale_mid,
                    moved,
                    *attn_w,
                ],
                [SMEM] * 2 + [VMEM] * (6 + len(later) + 8) + [HBM] * len(attn_w),
                attn_buffer,
                name="attend_back_far",
            )
            if late is not None:
                out_grad = after(out_grad, others[0])
                others.append(place.swap_zh(after(other_ffn[:, hidden : 2 * hidden], out_grad)))
                own_attn, other_attn = return_rows(place, *after(late_ends, out_grad))
            query_grad, same_sum_near, *near = launch(
                functools.partial(attend_back_body, half_slots, len(early), 0, False, []),
                [
                    shape((tokens, width), F32),
                    shape((heads, block), F32),
                    *[shape((tokens, 2 * width), F32)] * len(early),
                ],
                [spot, biases[layer], *common, *early, out_grad, deltas, query_grad],
                [SMEM] * 2 + [VMEM] * (6 + len(early) + 3),
                name="attend_back_near",
            )
            same_total = jnp.sum(same_sum, 1) + jnp.sum(same_sum_near, 1)
            bias_grads[layer] = jnp.stack([same_total, -same_total], 1)
            received = [place.swap_dp(piece, place.s_bits) for piece in sent]
            for index in range(place.s_bits + 1, k):
                near = [a + b.astype(F32) for a, b in zip(near, received)]
                middle_at = len(near) // 2
                received = [
                    place.swap_dp(piece.astype(LOW), index) for piece in near[middle_at:]
                ]
                near = near[:middle_at]
            if late is not None:
                received = after(received, others[1], other_attn)
                others.append(place.swap_zh(after(other_ffn[:, 2 * hidden :], received)))
            three, *sums = launch(
                functools.partial(qkv_back_body, attn_lay, 1),
                [shape((tokens, 3 * width), LOW), *parts],
                [spot, query_grad, near[0], cosine, sine, received[0], *attn_w],
                [SMEM] + [VMEM] * 5 + [HBM] * len(attn_w),
                attn_buffer,
                name="qkv_back",
            )
            if late is not None:
                sums = after(sums, others[2])
                others.append(place.swap_zh(after(other_attn, sums)))
            attn_grads = functools.partial(
                weight_grads_of,
                True,
                ((0, 1), (2, 3)),
                [normed, three, middle_full, attended],
                4 * width,
                "attn_weights",
            )

            def attn_side(sent):
                partial = attn_grads(sent)
                if late is None:
                    return partial, None
                rows = return_rows(place, *after(ffn_rows, sent))
                return after(partial, rows), rows

            moved, pieces, attn_gain_grad, (attn_partial, last_rows) = step_back(
                sums, full, scale, gains[layer], middle, attn_side
            )
            pending = [*pieces, middle_full, full, scale, moved]
            gain_grads[layer] = (attn_gain_grad, ffn_gain_grad)
            if late is not None:
                last_own, last_other = last_rows
                last_sent = [place.swap_zh(after(last_other[:, :hidden], moved))]
                pieces = after(pieces, others[3])
                last_sent += [
                    place.swap_zh(after(last_other[:, i * hidden : (i + 1) * hidden], pieces))
                    for i in range(1, 3)
                ]
                keep_grads(
                    layer + 1,
                    own_ffn.astype(F32) + jnp.concatenate(others[:3], 1).astype(F32),
                    own_attn.astype(F32) + others[3].astype(F32),
                )
            sent, other_sent, *attn_kept = after(attn_partial, moved)
            late = (ffn_rows, scatter_start(place, sent, other_sent), attn_kept)

        mine = jnp.stack([gain_grads[layer][i] for i in range(2) for layer in range(LAYERS)])
        wide = lax.dynamic_update_slice_in_dim(
            jnp.zeros((2 * LAYERS, depth), F32), mine, own_quarter * quarter, 1
        )
        bias_wide = lax.dynamic_update_slice_in_dim(
            jnp.zeros((LAYERS, 4 * heads, 2), F32), jnp.stack(bias_grads), own_quarter * heads, 1
        )
        total = jnp.concatenate([wide.reshape(-1), bias_wide.reshape(-1)])
        total = after(total, *pending)
        total = total + place.swap_core(total)
        for i in range(k):
            total = total + place.swap_dp(total, i)
        total = total + place.swap_zl(total)
        total_zh = place.swap_zh(total)
        input_grad = natural_rows(pending[:4], pending[4:]).astype(F32)
        total = total + total_zh
        own_attn, other_attn = return_rows(place, *scatter_rest(place, *late[1:]))
        attn_out = own_attn.astype(F32) + place.swap_zh(other_attn).astype(F32)
        ffn_out = last_own.astype(F32) + jnp.concatenate(last_sent, 1).astype(F32)
        keep_grads(0, ffn_out, attn_out)
        wide = total[: wide.size].reshape(wide.shape)
        bias_wide = total[wide.size :].reshape(bias_wide.shape)
        tensor = 2 * place.zh + place.zl
        gains_out = lax.dynamic_slice_in_dim(wide, tensor * quarter, quarter, 1)
        bias_out = lax.dynamic_slice_in_dim(bias_wide, tensor * heads, heads, 1)
        stacks = [
            jnp.stack([weight_grads[layer][member] for layer in range(LAYERS)])
            for member in range(7)
        ]
        return (output, input_grad, *stacks, gains_out[:LAYERS], gains_out[LAYERS:], bias_out)

    return run


def solution(mesh):
    n_ctx = mesh.shape["ctx"]
    dims = (mesh.shape["shard"], n_ctx // 2, 2, 2, mesh.shape["tensor"] // 2)
    mesh = jax.sharding.Mesh(mesh.devices.reshape(dims), AXES)
    ctx, tensor = ("o", "c"), ("zh", "zl")
    column = P(None, ("shard", "o", "c"), tensor)
    row = P(None, tensor, ("shard", "o", "c"))
    tokens = P(ctx, "shard", tensor)
    gain = P(None, tensor)
    bias = P(None, tensor, None)
    return jax.shard_map(
        per_device(Place(mesh)),
        mesh=mesh,
        in_specs=(
            tokens, column, column, column, row, column, column, row,
            gain, gain, bias, P("shard"), P(ctx, "shard"), tokens,
        ),
        out_specs=(
            tokens, tokens, column, column, column, row, column, column, row, gain, gain, bias,
        ),
        check_vma=False,
    )
```

```python
import functools

import jax
import jax.numpy as jnp
from jax import lax
from jax.experimental import pallas as pl
from jax.experimental.pallas import tpu as pltpu
from jax.sharding import PartitionSpec as P

HD = 64
LAYERS = 2
epsilon = 1e-06
masked = -1e30
F32 = jnp.float32
LOW = jnp.bfloat16
AXES = ("shard", "o", "c", "zh", "zl")


def bits_of(count):
    width = count.bit_length() - 1
    assert 1 << width == count
    return width


def dot(left, right, left_dim, right_dim):
    return lax.dot_general(
        left, right, (((left_dim,), (right_dim,)), ((), ())), preferred_element_type=F32
    )


class Place:
    def __init__(self, mesh):
        self.n_shard = mesh.shape["shard"]
        self.n_o = mesh.shape["o"]
        self.n_ctx = 2 * self.n_o
        assert mesh.shape["zh"] == mesh.shape["zl"] == 2
        self.s_bits = bits_of(self.n_shard)
        self.o_bits = bits_of(self.n_o)
        self.dp = [("s", i) for i in reversed(range(self.s_bits))] + [
            ("o", i) for i in reversed(range(self.o_bits))
        ]

    def locate(self):
        self.zh = lax.axis_index("zh")
        self.zl = lax.axis_index("zl")
        self.s = lax.axis_index("shard")
        self.o = lax.axis_index("o")
        self.c = lax.axis_index("c")
        self.dp_bit = [((self.s if kind == "s" else self.o) >> i) & 1 for kind, i in self.dp]

    def away(self, bits):
        away_s = away_o = 0
        for bit, (kind, i) in zip(bits, self.dp):
            if kind == "s":
                away_s |= bit << i
            else:
                away_o |= bit << i
        return away_s, away_o

    def move(self, array, route):
        pairs = []
        for shard in range(self.n_shard):
            for ctx in range(self.n_ctx):
                for tensor in range(4):
                    s, o, c, zh, zl = route(shard, ctx // 2, ctx % 2, tensor // 2, tensor % 2)
                    source = (shard * self.n_ctx + ctx) * 4 + tensor
                    target = (s * self.n_ctx + 2 * o + c) * 4 + 2 * zh + zl
                    pairs.append((source, target))
        return lax.ppermute(array, AXES, pairs)

    def swap_core(self, array):
        return self.move(array, lambda s, o, c, zh, zl: (s, o, 1 - c, zh, zl))

    def swap_zl(self, array):
        return self.move(array, lambda s, o, c, zh, zl: (s, o, c, zh, 1 - zl))

    def swap_zh(self, array):
        return self.move(array, lambda s, o, c, zh, zl: (s, o, c, 1 - zh, zl))

    def swap_dp(self, array, index):
        kind, i = self.dp[index]
        if kind == "s":
            return self.move(array, lambda s, o, c, zh, zl: (s ^ (1 << i), o, c, zh, zl))
        return self.move(array, lambda s, o, c, zh, zl: (s, o ^ (1 << i), c, zh, zl))

    def near(self, array):
        return self.move(array, lambda s, o, c, zh, zl: (s, o, zh, c, zl))

    def far(self, array):
        return self.move(array, lambda s, o, c, zh, zl: (s, o, zh, 1 - c, zl))

    def far_back(self, array):
        return self.move(array, lambda s, o, c, zh, zl: (s, o, 1 - zh, c, zl))


def flip_if(bit, array, axis):
    return jnp.where(bit == 1, jnp.flip(array, axis), array)


def pick(flag, one, two):
    return jnp.where(flag == 1, one, two)


VMEM = pl.BlockSpec(memory_space=pltpu.VMEM)
SMEM = pl.BlockSpec(memory_space=pltpu.SMEM)
HBM = pl.BlockSpec(memory_space=pl.ANY)
MIB = 1024 * 1024
WORK = {
    "frame": 2,
    "qkv": 5,
    "attend": 8,
    "ffn": 9,
    "ffn_back": 10,
    "ffn_both": 12,
    "ffn_weights": 9,
    "attend_back_far": 9,
    "attend_back_near": 6,
    "qkv_back": 5,
    "attn_weights": 4,
    "leave": 3,
}


def shape(dims, kind):
    return jax.ShapeDtypeStruct(dims, kind)


def launch(body, outs, operands, specs, scratch=(), name=None):
    return pl.pallas_call(
        body,
        out_shape=outs,
        in_specs=specs,
        out_specs=[VMEM] * len(outs),
        scratch_shapes=list(scratch),
        compiler_params=pltpu.CompilerParams(vmem_limit_bytes=52 * MIB),
        cost_estimate=pl.CostEstimate(
            flops=int(WORK[name] * 1.15e9), bytes_accessed=1024, transcendentals=0
        ),
        name=name,
    )(*operands)


def load_rows(pieces, layout, spot, buffer, sems):
    copies = []
    for array, row, count, target, col in layout:
        source = pieces[array].at[pl.ds(pl.multiple_of(row(spot), count), count)]
        here = buffer.at[
            pl.ds(pl.multiple_of(target(spot), count), count),
            pl.ds(col, pieces[array].shape[1]),
        ]
        copies.append(pltpu.make_async_copy(source, here, sems.at[len(copies)]))
    for copy in copies:
        copy.start()
    return copies


def feature_start(spot, dc, dz, width):
    return pl.multiple_of((2 * (spot[0] ^ dc) + (spot[1] ^ dz)) * width, width)


def join_feats(spot, pieces, full):
    width = pieces[0].shape[1]
    for i, piece in enumerate(pieces):
        full[:, pl.ds(feature_start(spot, i // 2, i % 2, width), width)] = piece[...]


def each_rows(total, step, body):
    step = min(step, total)

    for start in range(0, total, step):
        body(slice(start, start + step))


def norm_rows(full, gain, normed, scale):
    def one(rows):
        x = full[rows, :].astype(F32)
        r = lax.rsqrt(jnp.mean(x * x, axis=1, keepdims=True) + epsilon)
        scale[rows, :] = r
        normed[rows, :] = (x * r * gain[...]).astype(LOW)

    each_rows(full.shape[0], 128, one)


def finish_back(spot, pieces, before_full, rows_full, scale, moved, full, own):
    width = moved.shape[1]
    depth = full.shape[1]
    join_feats(spot, pieces, full)
    start = feature_start(spot, 0, 0, width)

    def one(rows):
        u = full[rows, :].astype(F32)
        n = rows_full[rows, :].astype(F32) * scale[rows, :]
        dots = jnp.sum((u - before_full[rows, :].astype(F32)) * n, axis=1, keepdims=True)
        dots = dots * (1.0 / depth)
        full[rows, :] = (u - n * dots).astype(LOW)
        mine = rows_full[rows, pl.ds(start, width)].astype(F32) * scale[rows, :]
        own[rows, :] = moved[rows, :] - mine * dots

    each_rows(full.shape[0], 128, one)


def turn(values, cosine, sine):
    width = values.shape[1]
    lane = lax.broadcasted_iota(jnp.int32, values.shape, 1) % HD
    other = jnp.where(
        lane < HD // 2, pltpu.roll(values, width - HD // 2, 1), pltpu.roll(values, HD // 2, 1)
    )
    return values * cosine + other * sine


def store_parts(parts, spot, product, width):
    for i, part in enumerate(parts):
        part[...] = product(feature_start(spot, i // 2, i % 2, width)).astype(part.dtype)


def part_shapes(tokens, width):
    return [shape((tokens, width), LOW)] * 4


def qkv_body(layout, joined, spot, *rest):
    pieces, rest = rest[: 1 if joined else 4], rest[1 if joined else 4 :]
    gain, cosine, sine = rest[:3]
    rest = rest[3:]
    count = 1 + max(entry[0] for entry in layout)
    weights = rest[:count]
    rest = rest[count:]
    if joined:
        full = pieces[0]
    else:
        full, rest = rest[0], rest[1:]
    normed, scale, queries, key_value, buffer, sems = rest
    copies = load_rows(weights, layout, spot, buffer, sems)
    if not joined:
        join_feats(spot, pieces, full)
    norm_rows(full, gain, normed, scale)
    for copy in copies:
        copy.wait()
    width = queries.shape[1]
    for i in range(3):
        product = dot(normed[...], buffer[:, i * width : (i + 1) * width], 1, 0)
        if i < 2:
            product = turn(product, cosine[...], sine[...])
        if i == 0:
            queries[...] = (product * 0.125).astype(LOW)
        else:
            key_value[:, (i - 1) * width : i * width] = product.astype(LOW)


def scores_of(q, k, same, row, step):
    return dot(q, k, 1, 1) + row + jnp.where(same, step, 0.0)


def attend_body(slots, n_blocks, layout, spot, bias, queries, own_kinds, kinds, masks, *rest):
    count = 1 + max(entry[0] for entry in layout)
    blocks = rest[:n_blocks]
    weights = rest[n_blocks : n_blocks + count]
    attended, logs, part0, part1, part2, part3, buffer, sems = rest[n_blocks + count :]
    copies = load_rows(weights, layout, spot, buffer, sems)
    tokens, width = queries.shape
    heads = width // HD
    size = tokens // slots
    wide = 2 * HD
    chunk = min(size, 256)
    side = lax.broadcasted_iota(jnp.int32, (1, wide), 1) // HD
    for slot in range(slots):
        keys = pl.ds(slot * size, size)
        for start in range(0, size, chunk):
            rows = pl.ds(slot * size + start, chunk)
            same = [
                own_kinds[rows, :] == kinds[slot : slot + 1, b * size : (b + 1) * size]
                for b in range(n_blocks)
            ]
            for pair in range(heads // 2):
                cols = slice(pair * wide, (pair + 1) * wide)
                values = slice(width + pair * wide, width + (pair + 1) * wide)
                both = queries[rows, cols]
                results = []
                for half in range(2):
                    head = 2 * pair + half
                    q = jnp.where(side == half, both, jnp.zeros_like(both))
                    step = bias[2 * head] - bias[2 * head + 1]
                    base = bias[2 * head + 1]
                    scores = [
                        scores_of(
                            q,
                            blocks[b][keys, cols],
                            same[b],
                            masks[slot : slot + 1, b * size : (b + 1) * size] + base,
                            step,
                        )
                        for b in range(n_blocks)
                    ]
                    highest = functools.reduce(
                        jnp.maximum, [jnp.max(s, axis=1, keepdims=True) for s in scores]
                    )
                    powers = [jnp.exp(s - highest) for s in scores]
                    total = functools.reduce(
                        lambda a, b: a + b, [jnp.sum(p, axis=1, keepdims=True) for p in powers]
                    )
                    product = functools.reduce(
                        lambda a, b: a + b,
                        [
                            dot(powers[b].astype(LOW), blocks[b][keys, values], 1, 0)
                            for b in range(n_blocks)
                        ],
                    )
                    results.append(product * (1.0 / total))
                    logs[rows, head : head + 1] = highest + jnp.log(total)
                attended[rows, cols] = jnp.where(side == 0, results[0], results[1]).astype(LOW)
    for copy in copies:
        copy.wait()
    share = part0.shape[1]
    last = slice(3 * width, 4 * width)
    store_parts(
        (part0, part1, part2, part3),
        spot,
        lambda start: dot(attended[...], buffer[pl.ds(start, share), last], 1, 1),
        share,
    )


def ffn_body(layout, spot, p0, p1, p2, p3, gain, *rest):
    count = 1 + max(entry[0] for entry in layout)
    weights = rest[:count]
    full, normed, scale, gate, up, hid, part0, part1, part2, part3, buffer, sems = rest[count:]
    copies = load_rows(weights, layout, spot, buffer, sems)
    join_feats(spot, (p0, p1, p2, p3), full)
    norm_rows(full, gain, normed, scale)
    for copy in copies:
        copy.wait()
    hidden = hid.shape[1]
    tile = 256

    for start in range(0, hidden, tile):
        here = slice(start, start + tile)
        g = dot(normed[...], buffer[:, here], 1, 0)
        u = dot(normed[...], buffer[:, hidden + start : hidden + start + tile], 1, 0)
        gate[:, here] = g.astype(LOW)
        up[:, here] = u.astype(LOW)
        hid[:, here] = (g * jax.nn.sigmoid(g) * u).astype(LOW)
    share = part0.shape[1]
    store_parts(
        (part0, part1, part2, part3),
        spot,
        lambda start: dot(hid[...], buffer[pl.ds(start, share), 2 * hidden : 3 * hidden], 1, 1),
        share,
    )


def ffn_both_body(layout, spot, p0, p1, p2, p3, gain, upstream, *rest):
    count = 1 + max(entry[0] for entry in layout)
    weights = rest[:count]
    full, normed, scale, hid, gate_grad, up_grad = rest[count : count + 6]
    sums, sums_back = rest[count + 6 : count + 10], rest[count + 10 : count + 14]
    buffer, sems = rest[count + 14 :]
    copies = load_rows(weights, layout, spot, buffer, sems)
    join_feats(spot, (p0, p1, p2, p3), full)
    norm_rows(full, gain, normed, scale)
    for copy in copies:
        copy.wait()
    hidden = hid.shape[1]
    tile = 256
    for start in range(0, hidden, tile):
        here = slice(start, start + tile)
        g = dot(normed[...], buffer[:, here], 1, 0)
        u = dot(normed[...], buffer[:, hidden + start : hidden + start + tile], 1, 0)
        grad = dot(upstream[...], buffer[:, 2 * hidden + start : 2 * hidden + start + tile], 1, 0)
        sig = jax.nn.sigmoid(g)
        hid[:, here] = (g * sig * u).astype(LOW)
        gate_grad[:, here] = (grad * u * sig * (1.0 + g * (1.0 - sig))).astype(LOW)
        up_grad[:, here] = (grad * g * sig).astype(LOW)
    share = sums[0].shape[1]
    store_parts(
        sums_back,
        spot,
        lambda start: dot(gate_grad[...], buffer[pl.ds(start, share), :hidden], 1, 1)
        + dot(up_grad[...], buffer[pl.ds(start, share), hidden : 2 * hidden], 1, 1),
        share,
    )
    store_parts(
        sums,
        spot,
        lambda start: dot(hid[...], buffer[pl.ds(start, share), 2 * hidden : 3 * hidden], 1, 1),
        share,
    )


def ffn_back_body(finish, layout, spot, *rest):
    count = 1 + max(entry[0] for entry in layout)
    if finish:
        p0, p1, p2, p3, before_full, rows_full, scale, moved = rest[:8]
        rest = rest[8:]
    else:
        full_in = rest[0]
        rest = rest[1:]
    gate, up = rest[:2]
    weights = rest[2 : 2 + count]
    rest = rest[2 + count :]
    if finish:
        full, own = rest[:2]
        rest = rest[2:]
    gate_grad, up_grad, part0, part1, part2, part3, buffer, sems = rest
    copies = load_rows(weights, layout, spot, buffer, sems)
    if finish:
        finish_back(
            spot, (p0, p1, p2, p3), before_full, rows_full, scale, moved, full, own
        )
    else:
        full = full_in
    for copy in copies:
        copy.wait()
    hidden = gate.shape[1]
    tile = 256

    for start in range(0, hidden, tile):
        here = slice(start, start + tile)
        grad = dot(full[...], buffer[:, 2 * hidden + start : 2 * hidden + start + tile], 1, 0)
        g = gate[:, here].astype(F32)
        sig = jax.nn.sigmoid(g)
        gate_grad[:, here] = (
            grad * up[:, here].astype(F32) * sig * (1.0 + g * (1.0 - sig))
        ).astype(LOW)
        up_grad[:, here] = (grad * g * sig).astype(LOW)
    share = part0.shape[1]
    store_parts(
        (part0, part1, part2, part3),
        spot,
        lambda start: dot(gate_grad[...], buffer[pl.ds(start, share), :hidden], 1, 1)
        + dot(up_grad[...], buffer[pl.ds(start, share), hidden : 2 * hidden], 1, 1),
        share,
    )


def grad_columns(pairs, blocks, operands, rows, out, out_rows):
    col = 0
    for left, right in pairs:
        right = operands[right]
        width = right.shape[1]
        for start in range(0, width, 512):
            tile = min(512, width - start)
            out[out_rows, col : col + tile] = dot(
                blocks[left][:, rows], right[:, start : start + tile], 0, 0
            ).astype(LOW)
            col += tile


def arrange(operands, pairs, spot, order, scratch):
    blocks = {}
    for buffer, left in zip(scratch, sorted({left for left, _ in pairs})):
        width = buffer.shape[1] // len(order)
        for i, block in enumerate(order):
            at = pl.multiple_of(block(spot) * width, width)
            buffer[:, i * width : (i + 1) * width] = operands[left][:, pl.ds(at, width)]
        blocks[left] = buffer
    return blocks


def weight_grad_group_body(pairs, order, fit, spot, *refs):
    operands, (out,) = refs[: len(refs) - 1 - fit], refs[len(refs) - 1 - fit :][:1]
    blocks = arrange(operands, pairs, spot, order, refs[len(refs) - fit :]) if fit else operands
    step = min(256, out.shape[0])
    for start in range(0, out.shape[0], step):
        rows = slice(start, start + step)
        grad_columns(pairs, blocks, operands, rows, out, rows)


def relative_order(k):
    def bits(i):
        return [(i >> (k - 1 - j)) & 1 for j in range(k)]

    first = [(tuple(bits(i)), 0) for i in range(2**k)]
    second = [(tuple(reversed(bits(i))), 1) for i in range(2**k)]
    return first + second


def weight_grad_sent_body(pairs, order, fit, spot, *refs):
    operands, outs = refs[: len(refs) - 4 - fit], refs[len(refs) - 4 - fit :][:4]
    blocks = arrange(operands, pairs, spot, order, refs[len(refs) - fit :]) if fit else operands
    depth = outs[0].shape[0]
    for i, out in zip((1, 3, 0, 2), outs):
        rows = slice(i * depth, (i + 1) * depth)
        grad_columns(pairs, blocks, operands, rows, out, slice(0, depth))


def attend_back_body(
    slots, n_blocks, first_block, first, layout, spot, bias, queries, attended, logs, *rest
):
    count = 1 + max([entry[0] for entry in layout] + [-1])
    own_kinds, kinds, masks = rest[:3]
    blocks = rest[3 : 3 + n_blocks]
    rest = rest[3 + n_blocks :]
    tokens, width = queries.shape
    if first:
        p0, p1, p2, p3, before_full, rows_full, scale, moved = rest[:8]
        weights = rest[8 : 8 + count]
        full, own, out_grad, deltas, query_grad, same_sum = rest[8 + count : 14 + count]
        grads = rest[14 + count : 14 + count + n_blocks]
        buffer, sems = rest[14 + count + n_blocks :]
        copies = load_rows(weights, layout, spot, buffer, sems)
        finish_back(
            spot, (p0, p1, p2, p3), before_full, rows_full, scale, moved, full, own
        )
        for copy in copies:
            copy.wait()
        out_grad[...] = dot(full[...], buffer[:, 3 * width :], 1, 0).astype(LOW)
    else:
        out_grad, deltas, query_before = rest[:3]
        query_grad, same_sum = rest[3:5]
        grads = rest[5 : 5 + n_blocks]
    heads = width // HD
    size = tokens // slots
    wide = 2 * HD
    side = lax.broadcasted_iota(jnp.int32, (1, wide), 1) // HD
    if first:
        for head in range(heads):
            cols = slice(head // 2 * wide, (head // 2 + 1) * wide)
            product = attended[:, cols].astype(F32) * out_grad[:, cols].astype(F32)
            deltas[:, head : head + 1] = jnp.sum(
                jnp.where(side == head % 2, product, 0.0), axis=1, keepdims=True
            )
    same_sum[...] = jnp.zeros_like(same_sum)
    for slot in range(slots):
        keys = pl.ds(slot * size, size)
        for pair in range(heads // 2):
            cols = slice(pair * wide, (pair + 1) * wide)
            values = slice(width + pair * wide, width + (pair + 1) * wide)
            both = queries[keys, cols]
            grad_both = out_grad[keys, cols]
            query_total = None
            for b in range(n_blocks):
                place_b = first_block + b
                these = slice(place_b * size, (place_b + 1) * size)
                same = own_kinds[keys, :] == kinds[slot : slot + 1, these]
                k = blocks[b][keys, cols]
                v = blocks[b][keys, values]
                key_total = value_total = None
                for half in range(2):
                    head = 2 * pair + half
                    q = jnp.where(side == half, both, jnp.zeros_like(both))
                    g = jnp.where(side == half, grad_both, jnp.zeros_like(both))
                    step = bias[2 * head] - bias[2 * head + 1]
                    base = bias[2 * head + 1]
                    scores = scores_of(q, k, same, masks[slot : slot + 1, these] + base, step)
                    soft = jnp.exp(scores - logs[keys, head : head + 1])
                    soft_grad = dot(g, v, 1, 1)
                    score_grad = soft * (soft_grad - deltas[keys, head : head + 1])
                    same_sum[head : head + 1, :] += jnp.sum(
                        jnp.where(same, score_grad, 0.0), axis=0, keepdims=True
                    )
                    low = score_grad.astype(LOW)
                    masked_k = jnp.where(side == half, k, jnp.zeros_like(k))
                    query_part = dot(low, masked_k, 1, 0)
                    key_part = dot(low, q, 0, 0)
                    value_part = dot(soft.astype(LOW), g, 0, 0)
                    query_total = query_part if query_total is None else query_total + query_part
                    key_total = key_part if key_total is None else key_total + key_part
                    value_total = value_part if value_total is None else value_total + value_part
                grads[b][keys, cols] = key_total.astype(grads[b].dtype)
                grads[b][keys, values] = value_total.astype(grads[b].dtype)
            query_total = query_total * 0.125
            if not first:
                query_total = query_total + query_before[keys, cols]
            query_grad[keys, cols] = query_total


def qkv_back_body(layout, n_received, spot, query_grad, key_value, cosine, sine, *rest):
    count = 1 + max(entry[0] for entry in layout)
    received = rest[:n_received]
    weights = rest[n_received : n_received + count]
    three, part0, part1, part2, part3, buffer, sems = rest[n_received + count :]
    copies = load_rows(weights, layout, spot, buffer, sems)
    width = query_grad.shape[1]
    total = key_value[...]
    for other in received:
        total = total + other[...].astype(F32)
    three[:, :width] = turn(query_grad[...], cosine[...], -sine[...]).astype(LOW)
    three[:, width : 2 * width] = turn(total[:, :width], cosine[...], -sine[...]).astype(LOW)
    three[:, 2 * width :] = total[:, width:].astype(LOW)
    for copy in copies:
        copy.wait()
    share = part0.shape[1]
    store_parts(
        (part0, part1, part2, part3),
        spot,
        lambda start: dot(three[...], buffer[pl.ds(start, share), : 3 * width], 1, 1),
        share,
    )


def frame_body(slots, masked_rows, table, spot, mine, other, *rest):
    valid, full = (rest[0], rest[1]) if masked_rows else (None, rest[0])
    positions = mine.shape[2]
    blocks = table.shape[0]
    lanes = full.shape[1] // blocks
    for near in range(2):
        source = mine if near == 0 else other
        for slot in range(slots):
            start = pl.multiple_of((2 * slot + (spot[0] ^ near)) * positions, positions)
            for spot_out in range(blocks):
                block = table[spot_out]
                per = blocks // 4
                quarter = block // per
                which = (2 * ((quarter // 2) ^ spot[2])) + ((quarter % 2) ^ spot[1])
                lane = pl.multiple_of((block % per) * lanes, lanes)
                values = source[which, slot, :, pl.ds(lane, lanes)]
                if masked_rows:
                    values = values * valid[pl.ds(start, positions), :].astype(LOW)
                full[pl.ds(start, positions), spot_out * lanes : (spot_out + 1) * lanes] = values


def after(value, *others):
    return lax.optimization_barrier((value, others))[0]


def take_rows(place, natural, other):
    same = (place.c == place.zh).astype(jnp.int32)
    kept = pick(same, natural, other)
    received = place.swap_core(pick(same, other, natural))
    return pick(same, kept, received), pick(same, received, kept)


def return_rows(place, first, second):
    same = (place.c == place.zh).astype(jnp.int32)
    kept = pick(same, first, second)
    received = place.swap_core(pick(same, second, first))
    return pick(same, kept, received), pick(same, received, kept)


def gather_rows_swap(place, both, waits=()):
    k = len(place.dp)
    pieces, layout, early = [], [], []
    count = both[0].shape[0]
    for side, order in ((0, list(range(k))), (1, list(reversed(range(k))))):
        held, blocks = [both[side]], [(0,) * k]
        for index in order:
            send = held[0] if len(held) == 1 else jnp.concatenate(after(held, *waits), 0)
            held.append(place.swap_dp(send, index))
            if len(held) == 2:
                early.append(held[1])
            blocks += [b[:index] + (1 - b[index],) + b[index + 1 :] for b in blocks]
        at = 0
        for piece in held:
            for row in range(0, piece.shape[0], count):
                target = row_block(place, blocks[at], side)
                layout.append(
                    (
                        len(pieces),
                        lambda spot, row=row: row,
                        count,
                        lambda spot, target=target: target(spot) * count,
                        0,
                    )
                )
                at += 1
            pieces.append(piece)
    return pieces, layout, early


def row_block(place, bits, side):
    away_s, away_o = place.away(bits)
    chips = place.n_o
    return lambda spot: (
        ((spot[3] ^ away_s) * chips + (spot[4] ^ away_o)) * 2 + (spot[2] ^ side)
    )


def gather_rows_group(place, chunks):
    both = jnp.concatenate(
        [jnp.concatenate([chunk[side] for chunk in chunks], 1) for side in range(2)], 0
    )
    rows = lax.all_gather(both, ("shard", "o"), axis=0, tiled=True)
    chips = place.n_shard * place.n_o
    count = rows.shape[0] // (2 * chips)
    layout = [
        (
            0,
            lambda spot, i=i: i * count,
            count,
            lambda spot, i=i: (i - i % 2 + (i % 2 ^ spot[2])) * count,
            0,
        )
        for i in range(2 * chips)
    ]
    return [rows], layout


def join_chunks(*chunks):
    arrays, layout, column = [], [], 0
    for pieces, lay in chunks:
        layout += [(a + len(arrays), row, count, target, column) for a, row, count, target, _ in lay]
        arrays = arrays + pieces
        column += pieces[0].shape[1]
    return arrays, layout


def scatter_rows_group(place, partial):
    rows = lax.psum_scatter(partial, ("shard", "o"), scatter_dimension=0, tiled=True)
    half = rows.shape[0] // 2
    return rows[:half], rows[half:]


def scatter_start(place, sent, other_sent):
    return place.swap_dp(sent, 0), place.swap_dp(other_sent, len(place.dp) - 1)


def scatter_next(place, received, kept, step):
    k = len(place.dp)
    parts = [(a.astype(F32) + b.astype(F32)).astype(LOW) for a, b in zip(kept, received)]
    if step == k:
        return parts, None
    middle = parts[0].shape[0] // 2
    got = [
        place.swap_dp(parts[0][middle:], step),
        place.swap_dp(parts[1][middle:], k - 1 - step),
    ]
    return got, [part[:middle] for part in parts]


def scatter_rest(place, received, kept, step=1):
    while kept is not None:
        received, kept = scatter_next(place, received, kept, step)
        step += 1
    return received


def gather_feats(place, share):
    other = place.swap_zl(share)
    return [share, other, place.swap_core(share), place.swap_core(other)]


def scatter_feats(place, parts, beside=None):
    kept, kept_pair, sent, sent_pair = parts
    middle = (kept_pair.astype(F32) + place.swap_core(sent_pair).astype(F32)).astype(LOW)
    near = kept.astype(F32) + place.swap_core(sent).astype(F32)
    received = place.swap_zl(middle)
    done = None if beside is None else beside(middle)
    return near + after(received, done).astype(F32), done


def gather_keys(place, own):
    pieces = [own]
    for index in reversed(range(place.s_bits, len(place.dp))):
        pieces = pieces + [place.swap_dp(piece, index) for piece in pieces]
    return pieces


def per_device(place):
    def run(
        inputs,
        w_query,
        w_key,
        w_value,
        w_out,
        w_gate,
        w_up,
        w_down,
        attn_gain,
        ffn_gain,
        variate_bias,
        lengths,
        variates,
        cotangent,
    ):
        place.locate()
        positions, slots, quarter = inputs.shape
        depth = quarter * 4
        half_slots = slots // 2
        block = 2 * positions
        n_o = place.n_ctx // 2
        tokens = half_slots * block
        width = w_query.shape[2]
        heads = width // HD
        hidden = w_gate.shape[2]
        own_quarter = 2 * place.c + place.zl
        spot = jnp.stack([place.c, place.zl, place.zh, place.s, place.o]).astype(jnp.int32)
        k = len(place.dp)
        n_blocks = 2 ** (k + 1)
        block_rows = depth // n_blocks
        table = jnp.arange(n_blocks, dtype=jnp.int32)
        block_rows = depth // n_blocks
        lanes_fit = block_rows % 128 == 0

        attn_packs = [
            jnp.concatenate([w_query[i], w_key[i], w_value[i], w_out[i].T], 1)
            for i in range(LAYERS)
        ]

        def swap_slots(natural):
            first, second = natural[:, :half_slots], natural[:, half_slots:]
            return place.swap_zh(pick(place.zh, first, second).transpose(1, 0, 2))

        def two_quarters(natural, received):
            first, second = natural[:, :half_slots], natural[:, half_slots:]
            own = pick(place.zh, second, first).transpose(1, 0, 2)
            return jnp.stack([own, received])

        def four_quarters(two, other):
            return jnp.stack([two, other], 1).reshape(4, half_slots, positions, quarter)

        def token_rows(quarters, valid):
            mine, other = quarters[:2]
            if lanes_fit:
                operands = [table, spot, mine, other] + ([] if valid is None else [valid])
                return launch(
                    functools.partial(frame_body, half_slots, valid is not None),
                    [shape((tokens, depth), LOW)],
                    operands,
                    [SMEM, SMEM] + [VMEM] * (len(operands) - 2),
                    name="frame",
                )[0]
            by_core = jnp.stack([pick(place.c, other, mine), pick(place.c, mine, other)], 0)
            cut = by_core.reshape(2, 2, 2, half_slots, positions, quarter)
            cut = flip_if(place.zl, flip_if(place.zh, cut, 1), 2)
            rows = cut.transpose(3, 0, 4, 1, 2, 5).reshape(tokens, depth)
            return rows if valid is None else rows * valid.astype(LOW)

        def leave_rows(rows):
            cut = rows.reshape(half_slots, 2, positions, quarter)
            same = (place.c == place.zh).astype(jnp.int32)
            kept = pick(place.c, cut[:, 1], cut[:, 0])
            other = place.swap_core(pick(place.c, cut[:, 0], cut[:, 1]))
            mine = pick(same, kept, other)
            received = place.swap_zh(pick(same, other, kept))
            both = jnp.concatenate(
                [pick(place.zh, received, mine), pick(place.zh, mine, received)], 0
            )
            return both.transpose(1, 0, 2)

        zh_done = swap_slots(inputs)
        two = two_quarters(inputs, zh_done)
        zl_done = place.swap_zl(two)
        mine = four_quarters(two, zl_done)
        other = place.swap_core(mine)
        small = jnp.concatenate(
            [attn_gain.reshape(-1), ffn_gain.reshape(-1), variate_bias.reshape(-1)]
        ).reshape(1, -1)
        small = after(small, zh_done)
        pair = jnp.stack([small, place.swap_zh(small)], 0)
        all_small = jnp.stack([pair, place.swap_zl(pair)], 2)
        all_small = flip_if(place.zl, flip_if(place.zh, all_small, 0), 2)
        small = all_small.reshape(4, -1)
        cut = LAYERS * quarter
        natural_gains = jnp.concatenate(
            [
                small[:, i * cut : (i + 1) * cut]
                .reshape(4, LAYERS, quarter)
                .transpose(1, 0, 2)
                .reshape(LAYERS, depth)
                for i in range(2)
            ]
        )
        gains = natural_gains
        biases = lax.dynamic_index_in_dim(
            small[:, 2 * cut :].reshape(4, LAYERS, 2 * heads), own_quarter, 0, keepdims=False
        )

        ffn_chunks = [(w_gate[i], w_up[i], w_down[i].T) for i in range(LAYERS)]

        def take_late(natural, start, use):
            natural = after(natural, start)
            return take_rows(place, natural, after(place.swap_zh(natural), use))

        attn_both = take_late(attn_packs[0], zh_done, zh_done)
        gate = after(ffn_chunks[0][0], attn_both)
        gate_other = place.swap_zh(gate)
        *first_attn, early = gather_rows_swap(place, attn_both)
        up = after(ffn_chunks[0][1], early)
        up_other = place.swap_zh(up)

        own_kinds = after(variates.astype(F32), zl_done)
        rest = place.swap_core(own_kinds)
        own_kinds = jnp.concatenate(
            [pick(place.c, rest, own_kinds), pick(place.c, own_kinds, rest)], 0
        )
        own_kinds = pick(place.zh, own_kinds[:, half_slots:], own_kinds[:, :half_slots]).T
        kinds = jnp.concatenate(gather_keys(place, own_kinds), 1)
        own_kinds = own_kinds.reshape(tokens, 1)
        own_lengths = pick(place.zh, lengths[half_slots:], lengths[:half_slots])
        own_positions = place.o * block + jnp.arange(block, dtype=jnp.int32)
        chips = jnp.arange(n_o, dtype=jnp.int32) ^ place.o
        key_positions = (
            chips[:, None] * block + jnp.arange(block, dtype=jnp.int32)[None, :]
        ).reshape(-1)
        masks = jnp.where(key_positions[None, :] < own_lengths[:, None], 0.0, masked).astype(F32)
        valid = (own_positions[None, :] < own_lengths[:, None]).astype(F32).reshape(tokens, 1)
        index = jnp.arange(width, dtype=jnp.int32) % HD
        inverse = 10000.0 ** (-(2.0 * (index % (HD // 2)).astype(F32)) / HD)
        angles = own_positions.astype(F32)[:, None] * inverse[None, :]
        cosine = jnp.tile(jnp.cos(angles), (half_slots, 1))
        sine = jnp.tile(
            jnp.where(index < HD // 2, -1.0, 1.0)[None, :] * jnp.sin(angles), (half_slots, 1)
        )

        def share_of(rows):
            return lax.dynamic_slice_in_dim(rows, own_quarter * quarter, quarter, -1)

        attn_buffer = [
            pltpu.VMEM((depth, 4 * width), LOW),
            pltpu.SemaphoreType.DMA((n_blocks,)),
        ]
        ffn_buffer = [
            pltpu.VMEM((depth, 3 * hidden), LOW),
            pltpu.SemaphoreType.DMA((2 * n_blocks,)),
        ]
        rows_low = shape((tokens, depth), LOW)
        column = shape((tokens, 1), F32)
        share_f32 = shape((tokens, quarter), F32)
        parts = part_shapes(tokens, quarter)

        if lanes_fit:
            full = launch(
                functools.partial(frame_body, half_slots, False),
                [rows_low],
                [table, spot, mine, other],
                [SMEM, SMEM, VMEM, VMEM],
                name="frame",
            )[0]
        else:
            by_core = jnp.stack([pick(place.c, other, mine), pick(place.c, mine, other)], 0)
            cut4 = by_core.reshape(2, 2, 2, half_slots, positions, quarter)
            cut4 = flip_if(place.zl, flip_if(place.zh, cut4, 1), 2)
            full = cut4.transpose(3, 0, 4, 1, 2, 5).reshape(tokens, depth)

        pieces = [full]
        current = share_of(full).astype(F32)
        kept, weights = [], []
        attn_w, attn_lay = first_attn
        nothing = ()
        for layer in range(LAYERS):
            first, more = layer == 0, layer + 1 < LAYERS
            outs = launch(
                functools.partial(qkv_body, attn_lay, layer == 0),
                ([] if layer == 0 else [rows_low])
                + [
                    rows_low,
                    column,
                    shape((tokens, width), LOW),
                    shape((tokens, 2 * width), LOW),
                ],
                [spot, *pieces, gains[layer : layer + 1], cosine, sine, *attn_w],
                [SMEM] + [VMEM] * (3 + len(pieces)) + [HBM] * len(attn_w),
                attn_buffer,
                name="qkv",
            )
            if layer > 0:
                full, outs = outs[0], outs[1:]
            normed, scale, queries, key_value = outs
            blocks = gather_keys(place, key_value)
            if first:
                gate_both = take_rows(place, gate, after(gate_other, key_value))
                up_both = take_rows(place, up, after(up_other, key_value))
                down = after(ffn_chunks[0][2], key_value)
                down_other = place.swap_zh(down)
                blocks = after(blocks, down_other, gate_both, up_both)
                gate_up = gather_rows_group(place, after((gate_both, up_both), blocks))
            if layer == LAYERS - 1:
                late_cotangent = after(cotangent, key_value)
                late_other = swap_slots(late_cotangent)
                blocks = after(blocks, late_other)
                late_two = two_quarters(after(late_cotangent, blocks), late_other)
                late_other = place.swap_zl(late_two)
            if more:
                attn_next = after(attn_packs[layer + 1], blocks)
                attn_other = place.swap_zh(attn_next)
            attended, logs, *sums = launch(
                functools.partial(attend_body, half_slots, n_o, attn_lay),
                [shape((tokens, width), LOW), shape((tokens, heads), F32), *parts],
                [spot, biases[layer], queries, own_kinds, kinds, masks, *blocks, *attn_w],
                [SMEM] * 2 + [VMEM] * (4 + n_o) + [HBM] * len(attn_w),
                attn_buffer,
                name="attend",
            )
            if more:
                sums = after(sums, attn_other)
                chunks = ffn_chunks[layer + 1]
                others = [place.swap_zh(after(chunks[0], sums))]
            if first:
                down_both = take_rows(place, down, after(down_other, attended))

            if layer == LAYERS - 1:
                sums = after(sums, late_other)
                late_mine = four_quarters(late_two, after(late_other, sums))
                late_other = place.swap_core(late_mine)

            def reduce_side(sent):
                return list(others) if more else [late_other]

            shared, _ = scatter_feats(place, sums, reduce_side)
            middle = current + shared
            if first:
                down_w, down_lay, early = gather_rows_swap(place, down_both, (middle,))
            mid_pieces = gather_feats(place, middle.astype(LOW))
            if layer == LAYERS - 1:
                upstream_full = token_rows((after(late_mine, middle), late_other), valid)
                mid_pieces = after(mid_pieces, upstream_full)
            if more:
                others.append(place.swap_zh(after(chunks[1], middle)))
                attn_both = take_rows(place, attn_next, after(attn_other, middle))
                mid_pieces = after(mid_pieces, others[1], attn_both)
            if first:
                mid_pieces = after(mid_pieces, down_w)
                ffn_w, ffn_lay = join_chunks(gate_up, (down_w, down_lay))
            if more:
                others.append(place.swap_zh(after(chunks[2], mid_pieces)))
                next_w, next_lay, early = gather_rows_swap(
                    place, after(attn_both, mid_pieces, ffn_w), nothing
                )
            operands = [
                spot,
                *mid_pieces,
                gains[LAYERS + layer : LAYERS + layer + 1],
            ]
            specs = [SMEM] + [VMEM] * 5
            hidden_low = shape((tokens, hidden), LOW)
            if more:
                full_mid, normed_mid, scale_mid, gate, up, hid, *sums = launch(
                    functools.partial(ffn_body, ffn_lay),
                    [rows_low, rows_low, column, *[hidden_low] * 3, *parts],
                    [*operands, *ffn_w],
                    specs + [HBM] * len(ffn_w),
                    ffn_buffer,
                    name="ffn",
                )
            else:
                full_mid, normed_mid, scale_mid, hid, *outs = launch(
                    functools.partial(ffn_both_body, ffn_lay),
                    [rows_low, rows_low, column, *[hidden_low] * 3, *parts, *parts],
                    [*operands, upstream_full, *ffn_w],
                    specs + [VMEM] + [HBM] * len(ffn_w),
                    ffn_buffer,
                    name="ffn_both",
                )
                gate = up = None
                last_grads, sums, last_sums = outs[:2], outs[2:6], outs[6:]
            weights.append((attn_w, attn_lay, ffn_w, ffn_lay))
            if more:
                sums = after(sums, early, others[2])

            def take_side(sent):
                return [
                    take_rows(place, chunk, after(other, sent))
                    for chunk, other in zip(chunks, others)
                ]

            shared, ffn_both = scatter_feats(place, sums, take_side if more else None)
            if more:
                attn_w, attn_lay = next_w, next_lay
                ffn_w, ffn_lay = gather_rows_group(place, ffn_both)
            current = middle + shared
            kept.append(
                (
                    full,
                    normed,
                    scale,
                    queries,
                    blocks,
                    attended,
                    logs,
                    full_mid,
                    normed_mid,
                    scale_mid,
                    gate,
                    up,
                    hid,
                )
            )
            if more:
                pieces = gather_feats(place, current.astype(LOW))

        natural_valid = (
            ((2 * place.o + place.c) * positions + jnp.arange(positions, dtype=jnp.int32))[:, None]
            < lengths[None, :]
        )

        upstream = share_of(upstream_full).astype(F32)

        def step_back(sums, full_rows, row_scale, gain, before, beside, final=None):
            shared, done = scatter_feats(place, sums, beside)
            own_rows = share_of(full_rows).astype(F32) * row_scale
            gain_grad = jnp.sum(shared * own_rows, 0)
            part = shared * share_of(gain)[None, :]
            moved = before + row_scale * part
            if final:
                dots = jnp.sum(part * own_rows, 1)
                sums = final(gain_grad)
                other = place.swap_zl(jnp.concatenate([dots, sums]))
                dots = dots + other[:tokens]
                sums = jnp.stack([sums, other[tokens:]])
                other = place.swap_core(jnp.concatenate([dots, sums.reshape(-1)]))
                dots = (dots + other[:tokens]).reshape(tokens, 1) * (1.0 / depth)
                sums = jnp.stack([sums, other[tokens:].reshape(sums.shape)])
                sums = flip_if(place.c, flip_if(place.zl, sums, 1), 0)
                return moved, [moved - row_scale * own_rows * dots], sums, done
            return moved, gather_feats(place, moved.astype(LOW)), gain_grad, done

        sent_order = [row_block(place, bits, side) for bits, side in relative_order(k)]
        group_order = [
            lambda spot, i=i: i - i % 2 + (i % 2 ^ spot[2]) for i in range(n_blocks)
        ]

        def weight_grads_of(swapped, pairs, operands, columns, name, ready):
            operands = after(operands, ready)
            lefts = sorted({left for left, _ in pairs})
            order = sent_order if swapped else group_order
            scratch = []
            if lanes_fit:
                scratch = [pltpu.VMEM((tokens, depth), LOW) for _ in lefts]
            else:
                index = jnp.stack([block(spot) for block in order])
                operands = [
                    jnp.take(array.reshape(tokens, n_blocks, block_rows), index, axis=1).reshape(
                        tokens, depth
                    )
                    if i in lefts
                    else array
                    for i, array in enumerate(operands)
                ]
            return launch(
                functools.partial(
                    weight_grad_sent_body if swapped else weight_grad_group_body,
                    pairs,
                    order,
                    len(scratch),
                ),
                [shape((depth // 4, columns), LOW)] * 4
                if swapped
                else [shape((depth, columns), LOW)],
                [spot, *operands],
                [SMEM] + [VMEM] * len(operands),
                scratch,
                name=name,
            )

        weight_grads = [None] * LAYERS

        def keep_grads(layer, ffn_out, attn_out):
            attn_out, ffn_out = attn_out.astype(F32), ffn_out.astype(F32)
            weight_grads[layer] = (
                attn_out[:, :width],
                attn_out[:, width : 2 * width],
                attn_out[:, 2 * width : 3 * width],
                attn_out[:, 3 * width :].T,
                ffn_out[:, :hidden],
                ffn_out[:, hidden : 2 * hidden],
                ffn_out[:, 2 * hidden :].T,
            )

        late = None
        gain_grads = [None] * LAYERS
        bias_grads = [None] * LAYERS
        half_keys = max(n_o // 2, 1)
        pending = None
        for layer in reversed(range(LAYERS)):
            attn_w, attn_lay, ffn_w, ffn_lay = weights[layer]
            (
                full,
                normed,
                scale,
                queries,
                blocks,
                attended,
                logs,
                full_mid,
                normed_mid,
                scale_mid,
                gate,
                up,
                hid,
            ) = kept[layer]
            hidden_low = shape((tokens, hidden), LOW)
            if pending is None:
                (gate_grad, up_grad), sums = last_grads, last_sums
            else:
                upstream_full, upstream, gate_grad, up_grad, *sums = launch(
                    functools.partial(ffn_back_body, True, ffn_lay),
                    [rows_low, share_f32, hidden_low, hidden_low, *parts],
                    [spot, *pending, gate, up, *ffn_w],
                    [SMEM] + [VMEM] * 10 + [HBM] * len(ffn_w),
                    ffn_buffer,
                    name="ffn_back",
                )
            if late is not None:
                late_ffn, late_got, late_kept = late
                sums = after(sums, late_got)
            ffn_grads = functools.partial(
                weight_grads_of,
                False,
                ((0, 1), (0, 2), (3, 4)),
                [normed_mid, gate_grad, up_grad, upstream_full, hid],
                3 * hidden,
                "ffn_weights",
            )

            def ffn_side(sent):
                partial = ffn_grads(sent)
                if late is None:
                    return after(partial, current), None
                rows = return_rows(place, *after(late_ffn, sent))
                return after(partial, rows), rows

            moved, pieces, ffn_gain_grad, (ffn_partial, late_rows) = step_back(
                sums, full_mid, scale_mid, gains[LAYERS + layer], upstream, ffn_side
            )
            ffn_rows = scatter_rows_group(place, *ffn_partial)
            if late is not None:
                own_ffn, other_ffn = late_rows
                others = [place.swap_zh(after(other_ffn[:, :hidden], moved))]
                late_got, late_kept = scatter_next(place, after(late_got, moved), late_kept, 1)
                pieces = after(pieces, others[0], late_kept)
                others.append(place.swap_zh(after(other_ffn[:, hidden : 2 * hidden], pieces)))
            common = [queries, attended, logs, own_kinds, kinds, masks]
            later = blocks[half_keys:] if n_o > 1 else blocks
            early = blocks[:half_keys] if n_o > 1 else []
            start = half_keys if n_o > 1 else 0
            middle_full, middle, out_grad, deltas, query_grad, same_sum, *sent = launch(
                functools.partial(
                    attend_back_body, half_slots, len(later), start, True, attn_lay
                ),
                [
                    rows_low,
                    share_f32,
                    shape((tokens, width), LOW),
                    shape((tokens, heads), F32),
                    shape((tokens, width), F32),
                    shape((heads, block), F32),
                    *[shape((tokens, 2 * width), LOW)] * len(later),
                ],
                [
                    spot,
                    biases[layer],
                    *common,
                    *later,
                    *pieces,
                    upstream_full,
                    full_mid,
                    scale_mid,
                    moved,
                    *attn_w,
                ],
                [SMEM] * 2 + [VMEM] * (6 + len(later) + 8) + [HBM] * len(attn_w),
                attn_buffer,
                name="attend_back_far",
            )
            if layer == LAYERS - 1:
                output = leave_rows(after(current, moved).astype(LOW))
                output = output * natural_valid[:, :, None].astype(LOW)
                out_grad = after(out_grad, output)
            if late is not None:
                out_grad = after(out_grad, others[1], late_got)
                others.append(place.swap_zh(after(other_ffn[:, 2 * hidden :], out_grad)))
                late_ends = scatter_rest(place, after(late_got, out_grad), late_kept, 2)
                own_attn, other_attn = return_rows(place, *late_ends)
            query_grad, same_sum_near, *near = launch(
                functools.partial(attend_back_body, half_slots, len(early), 0, False, []),
                [
                    shape((tokens, width), F32),
                    shape((heads, block), F32),
                    *[shape((tokens, 2 * width), F32)] * len(early),
                ],
                [spot, biases[layer], *common, *early, out_grad, deltas, query_grad],
                [SMEM] * 2 + [VMEM] * (6 + len(early) + 3),
                name="attend_back_near",
            )
            same_total = jnp.sum(same_sum, 1) + jnp.sum(same_sum_near, 1)
            bias_grads[layer] = jnp.stack([same_total, -same_total], 1)
            received = [place.swap_dp(piece, place.s_bits) for piece in sent]
            for index in range(place.s_bits + 1, k):
                near = [a + b.astype(F32) for a, b in zip(near, received)]
                middle_at = len(near) // 2
                received = [
                    place.swap_dp(piece.astype(LOW), index) for piece in near[middle_at:]
                ]
                near = near[:middle_at]
            if late is not None:
                received = after(received, others[2], other_attn)
                others.append(place.swap_zh(after(other_attn, received)))
            three, *sums = launch(
                functools.partial(qkv_back_body, attn_lay, 1),
                [shape((tokens, 3 * width), LOW), *parts],
                [spot, query_grad, near[0], cosine, sine, received[0], *attn_w],
                [SMEM] + [VMEM] * 5 + [HBM] * len(attn_w),
                attn_buffer,
                name="qkv_back",
            )
            if late is not None:
                sums = after(sums, others[3])
            attn_grads = functools.partial(
                weight_grads_of,
                True,
                ((0, 1), (2, 3)),
                [normed, three, middle_full, attended],
                4 * width,
                "attn_weights",
            )

            def small_sums(gain_grad):
                gain_grads[0] = (gain_grad, ffn_gain_grad)
                mine = [gain_grads[i][j] for j in range(2) for i in range(LAYERS)]
                return jnp.concatenate([*mine, jnp.stack(bias_grads).reshape(-1)])

            def attn_side(sent):
                partial = attn_grads(sent)
                if late is None:
                    return partial, None
                rows = return_rows(place, *after(ffn_rows, sent))
                return after(partial, rows), rows

            moved, pieces, attn_gain_grad, (attn_partial, last_rows) = step_back(
                sums, full, scale, gains[layer], middle, attn_side, small_sums if layer == 0 else None
            )
            pending = [*pieces, middle_full, full, scale, moved]
            gain_grads[layer] = (attn_gain_grad, ffn_gain_grad)
            if late is not None:
                last_own, last_other = last_rows
                last_sent = place.swap_zh(after(last_other, moved))
                keep_grads(
                    layer + 1,
                    own_ffn.astype(F32) + jnp.concatenate(others[:3], 1).astype(F32),
                    own_attn.astype(F32) + others[3].astype(F32),
                )
            sent, other_sent, *attn_kept = after(attn_partial, moved)
            late = (ffn_rows, scatter_start(place, sent, other_sent), attn_kept)

        input_grad = leave_rows(pending[0].astype(LOW)).astype(F32)
        own_attn, other_attn = return_rows(place, *scatter_rest(place, *late[1:]))
        attn_out = own_attn.astype(F32) + place.swap_zh(other_attn).astype(F32)
        total = after(attn_gain_grad, other_attn)
        for i in range(k):
            total = total + place.swap_dp(total, i)
        total = total + place.swap_zh(total)
        small_cut = LAYERS * quarter
        total = total.reshape(4, -1)
        wide = total[:, : 2 * small_cut].reshape(4, 2 * LAYERS, quarter)
        bias_wide = total[:, 2 * small_cut :].reshape(4, LAYERS, heads, 2)
        ffn_out = last_own.astype(F32) + last_sent.astype(F32)
        keep_grads(0, ffn_out, attn_out)
        tensor = 2 * place.zh + place.zl
        gains_out = lax.dynamic_index_in_dim(wide, tensor, 0, keepdims=False)
        bias_out = lax.dynamic_index_in_dim(bias_wide, tensor, 0, keepdims=False)
        stacks = [
            jnp.stack([weight_grads[layer][member] for layer in range(LAYERS)])
            for member in range(7)
        ]
        return (output, input_grad, *stacks, gains_out[:LAYERS], gains_out[LAYERS:], bias_out)

    return run


def solution(mesh):
    n_ctx = mesh.shape["ctx"]
    dims = (mesh.shape["shard"], n_ctx // 2, 2, 2, mesh.shape["tensor"] // 2)
    mesh = jax.sharding.Mesh(mesh.devices.reshape(dims), AXES)
    ctx, tensor = ("o", "c"), ("zh", "zl")
    column = P(None, ("shard", "o", "c"), tensor)
    row = P(None, tensor, ("shard", "o", "c"))
    tokens = P(ctx, "shard", tensor)
    gain = P(None, tensor)
    bias = P(None, tensor, None)
    return jax.shard_map(
        per_device(Place(mesh)),
        mesh=mesh,
        in_specs=(
            tokens, column, column, column, row, column, column, row,
            gain, gain, bias, P("shard"), P(ctx, "shard"), tokens,
        ),
        out_specs=(
            tokens, tokens, column, column, column, row, column, column, row, gain, gain, bias,
        ),
        check_vma=False,
    )
```

```python
import functools

import jax
import jax.numpy as jnp
from jax import lax
from jax.experimental import pallas as pl
from jax.experimental.pallas import tpu as pltpu
from jax.sharding import PartitionSpec as P

HD = 64
LAYERS = 2
epsilon = 1e-06
masked = -1e30
F32 = jnp.float32
LOW = jnp.bfloat16
AXES = ("shard", "o", "c", "zh", "zl")


def bits_of(count):
    width = count.bit_length() - 1
    assert 1 << width == count
    return width


def dot(left, right, left_dim, right_dim):
    return lax.dot_general(
        left, right, (((left_dim,), (right_dim,)), ((), ())), preferred_element_type=F32
    )


class Place:
    def __init__(self, mesh):
        self.n_shard = mesh.shape["shard"]
        self.n_o = mesh.shape["o"]
        self.n_ctx = 2 * self.n_o
        assert mesh.shape["zh"] == mesh.shape["zl"] == 2
        self.s_bits = bits_of(self.n_shard)
        self.o_bits = bits_of(self.n_o)
        self.dp = [("s", i) for i in reversed(range(self.s_bits))] + [
            ("o", i) for i in reversed(range(self.o_bits))
        ]

    def locate(self):
        self.zh = lax.axis_index("zh")
        self.zl = lax.axis_index("zl")
        self.s = lax.axis_index("shard")
        self.o = lax.axis_index("o")
        self.c = lax.axis_index("c")
        self.dp_bit = [((self.s if kind == "s" else self.o) >> i) & 1 for kind, i in self.dp]

    def away(self, bits):
        away_s = away_o = 0
        for bit, (kind, i) in zip(bits, self.dp):
            if kind == "s":
                away_s |= bit << i
            else:
                away_o |= bit << i
        return away_s, away_o

    def move(self, array, route):
        pairs = []
        for shard in range(self.n_shard):
            for ctx in range(self.n_ctx):
                for tensor in range(4):
                    s, o, c, zh, zl = route(shard, ctx // 2, ctx % 2, tensor // 2, tensor % 2)
                    source = (shard * self.n_ctx + ctx) * 4 + tensor
                    target = (s * self.n_ctx + 2 * o + c) * 4 + 2 * zh + zl
                    pairs.append((source, target))
        return lax.ppermute(array, AXES, pairs)

    def swap_core(self, array):
        return self.move(array, lambda s, o, c, zh, zl: (s, o, 1 - c, zh, zl))

    def swap_zl(self, array):
        return self.move(array, lambda s, o, c, zh, zl: (s, o, c, zh, 1 - zl))

    def swap_zh(self, array):
        return self.move(array, lambda s, o, c, zh, zl: (s, o, c, 1 - zh, zl))

    def swap_dp(self, array, index):
        kind, i = self.dp[index]
        if kind == "s":
            return self.move(array, lambda s, o, c, zh, zl: (s ^ (1 << i), o, c, zh, zl))
        return self.move(array, lambda s, o, c, zh, zl: (s, o ^ (1 << i), c, zh, zl))

    def near(self, array):
        return self.move(array, lambda s, o, c, zh, zl: (s, o, zh, c, zl))

    def far(self, array):
        return self.move(array, lambda s, o, c, zh, zl: (s, o, zh, 1 - c, zl))

    def far_back(self, array):
        return self.move(array, lambda s, o, c, zh, zl: (s, o, 1 - zh, c, zl))


def flip_if(bit, array, axis):
    return jnp.where(bit == 1, jnp.flip(array, axis), array)


def pick(flag, one, two):
    return jnp.where(flag == 1, one, two)


VMEM = pl.BlockSpec(memory_space=pltpu.VMEM)
SMEM = pl.BlockSpec(memory_space=pltpu.SMEM)
HBM = pl.BlockSpec(memory_space=pl.ANY)
MIB = 1024 * 1024
WORK = {
    "frame": 2,
    "qkv": 5,
    "attend": 8,
    "ffn": 9,
    "ffn_back": 10,
    "ffn_both": 12,
    "ffn_weights": 9,
    "attend_back_far": 9,
    "attend_back_near": 6,
    "qkv_back": 5,
    "attn_weights": 4,
    "leave": 3,
}


def shape(dims, kind):
    return jax.ShapeDtypeStruct(dims, kind)


def launch(body, outs, operands, specs, scratch=(), name=None):
    return pl.pallas_call(
        body,
        out_shape=outs,
        in_specs=specs,
        out_specs=[VMEM] * len(outs),
        scratch_shapes=list(scratch),
        compiler_params=pltpu.CompilerParams(vmem_limit_bytes=52 * MIB),
        cost_estimate=pl.CostEstimate(
            flops=int(WORK[name] * 1.15e9), bytes_accessed=1024, transcendentals=0
        ),
        name=name,
    )(*operands)


def load_rows(pieces, layout, spot, buffer, sems):
    copies = []
    for array, row, count, target, col in layout:
        source = pieces[array].at[pl.ds(pl.multiple_of(row(spot), count), count)]
        here = buffer.at[
            pl.ds(pl.multiple_of(target(spot), count), count),
            pl.ds(col, pieces[array].shape[1]),
        ]
        copies.append(pltpu.make_async_copy(source, here, sems.at[len(copies)]))
    for copy in copies:
        copy.start()
    return copies


def feature_start(spot, dc, dz, width):
    return pl.multiple_of((2 * (spot[0] ^ dc) + (spot[1] ^ dz)) * width, width)


def join_feats(spot, pieces, full):
    width = pieces[0].shape[1]
    for i, piece in enumerate(pieces):
        full[:, pl.ds(feature_start(spot, i // 2, i % 2, width), width)] = piece[...]


def each_rows(total, step, body):
    step = min(step, total)

    for start in range(0, total, step):
        body(slice(start, start + step))


def norm_rows(full, gain, normed, scale):
    def one(rows):
        x = full[rows, :].astype(F32)
        r = lax.rsqrt(jnp.mean(x * x, axis=1, keepdims=True) + epsilon)
        scale[rows, :] = r
        normed[rows, :] = (x * r * gain[...]).astype(LOW)

    each_rows(full.shape[0], 128, one)


def finish_back(spot, pieces, before_full, rows_full, scale, moved, full, own):
    width = moved.shape[1]
    depth = full.shape[1]
    join_feats(spot, pieces, full)
    start = feature_start(spot, 0, 0, width)

    def one(rows):
        u = full[rows, :].astype(F32)
        n = rows_full[rows, :].astype(F32) * scale[rows, :]
        dots = jnp.sum((u - before_full[rows, :].astype(F32)) * n, axis=1, keepdims=True)
        dots = dots * (1.0 / depth)
        full[rows, :] = (u - n * dots).astype(LOW)
        mine = rows_full[rows, pl.ds(start, width)].astype(F32) * scale[rows, :]
        own[rows, :] = moved[rows, :] - mine * dots

    each_rows(full.shape[0], 128, one)


def turn(values, cosine, sine):
    width = values.shape[1]
    lane = lax.broadcasted_iota(jnp.int32, values.shape, 1) % HD
    other = jnp.where(
        lane < HD // 2, pltpu.roll(values, width - HD // 2, 1), pltpu.roll(values, HD // 2, 1)
    )
    return values * cosine + other * sine


def store_parts(parts, spot, product, width):
    for i, part in enumerate(parts):
        part[...] = product(feature_start(spot, i // 2, i % 2, width)).astype(part.dtype)


def part_shapes(tokens, width):
    return [shape((tokens, width), LOW)] * 4


def qkv_body(layout, joined, spot, *rest):
    pieces, rest = rest[: 1 if joined else 4], rest[1 if joined else 4 :]
    gain, cosine, sine = rest[:3]
    rest = rest[3:]
    count = 1 + max(entry[0] for entry in layout)
    weights = rest[:count]
    rest = rest[count:]
    if joined:
        full = pieces[0]
    else:
        full, rest = rest[0], rest[1:]
    normed, scale, queries, key_value, buffer, sems = rest
    copies = load_rows(weights, layout, spot, buffer, sems)
    if not joined:
        join_feats(spot, pieces, full)
    norm_rows(full, gain, normed, scale)
    for copy in copies:
        copy.wait()
    width = queries.shape[1]
    for i in range(3):
        product = dot(normed[...], buffer[:, i * width : (i + 1) * width], 1, 0)
        if i < 2:
            product = turn(product, cosine[...], sine[...])
        if i == 0:
            queries[...] = (product * 0.125).astype(LOW)
        else:
            key_value[:, (i - 1) * width : i * width] = product.astype(LOW)


def scores_of(q, k, same, row, step):
    return dot(q, k, 1, 1) + row + jnp.where(same, step, 0.0)


def attend_body(slots, n_blocks, layout, spot, bias, queries, own_kinds, kinds, masks, *rest):
    count = 1 + max(entry[0] for entry in layout)
    blocks = rest[:n_blocks]
    weights = rest[n_blocks : n_blocks + count]
    attended, logs, part0, part1, part2, part3, buffer, sems = rest[n_blocks + count :]
    copies = load_rows(weights, layout, spot, buffer, sems)
    tokens, width = queries.shape
    heads = width // HD
    size = tokens // slots
    wide = 2 * HD
    chunk = min(size, 256)
    side = lax.broadcasted_iota(jnp.int32, (1, wide), 1) // HD
    for slot in range(slots):
        keys = pl.ds(slot * size, size)
        for start in range(0, size, chunk):
            rows = pl.ds(slot * size + start, chunk)
            same = [
                own_kinds[rows, :] == kinds[slot : slot + 1, b * size : (b + 1) * size]
                for b in range(n_blocks)
            ]
            for pair in range(heads // 2):
                cols = slice(pair * wide, (pair + 1) * wide)
                values = slice(width + pair * wide, width + (pair + 1) * wide)
                both = queries[rows, cols]
                results = []
                for half in range(2):
                    head = 2 * pair + half
                    q = jnp.where(side == half, both, jnp.zeros_like(both))
                    step = bias[2 * head] - bias[2 * head + 1]
                    base = bias[2 * head + 1]
                    scores = [
                        scores_of(
                            q,
                            blocks[b][keys, cols],
                            same[b],
                            masks[slot : slot + 1, b * size : (b + 1) * size] + base,
                            step,
                        )
                        for b in range(n_blocks)
                    ]
                    highest = functools.reduce(
                        jnp.maximum, [jnp.max(s, axis=1, keepdims=True) for s in scores]
                    )
                    powers = [jnp.exp(s - highest) for s in scores]
                    total = functools.reduce(
                        lambda a, b: a + b, [jnp.sum(p, axis=1, keepdims=True) for p in powers]
                    )
                    product = functools.reduce(
                        lambda a, b: a + b,
                        [
                            dot(powers[b].astype(LOW), blocks[b][keys, values], 1, 0)
                            for b in range(n_blocks)
                        ],
                    )
                    results.append(product * (1.0 / total))
                    logs[rows, head : head + 1] = highest + jnp.log(total)
                attended[rows, cols] = jnp.where(side == 0, results[0], results[1]).astype(LOW)
    for copy in copies:
        copy.wait()
    share = part0.shape[1]
    last = slice(3 * width, 4 * width)
    store_parts(
        (part0, part1, part2, part3),
        spot,
        lambda start: dot(attended[...], buffer[pl.ds(start, share), last], 1, 1),
        share,
    )


def ffn_body(layout, spot, p0, p1, p2, p3, gain, *rest):
    count = 1 + max(entry[0] for entry in layout)
    weights = rest[:count]
    full, normed, scale, gate, up, hid, part0, part1, part2, part3, buffer, sems = rest[count:]
    copies = load_rows(weights, layout, spot, buffer, sems)
    join_feats(spot, (p0, p1, p2, p3), full)
    norm_rows(full, gain, normed, scale)
    for copy in copies:
        copy.wait()
    hidden = hid.shape[1]
    tile = 256

    for start in range(0, hidden, tile):
        here = slice(start, start + tile)
        g = dot(normed[...], buffer[:, here], 1, 0)
        u = dot(normed[...], buffer[:, hidden + start : hidden + start + tile], 1, 0)
        gate[:, here] = g.astype(LOW)
        up[:, here] = u.astype(LOW)
        hid[:, here] = (g * jax.nn.sigmoid(g) * u).astype(LOW)
    share = part0.shape[1]
    store_parts(
        (part0, part1, part2, part3),
        spot,
        lambda start: dot(hid[...], buffer[pl.ds(start, share), 2 * hidden : 3 * hidden], 1, 1),
        share,
    )


def ffn_both_body(layout, spot, p0, p1, p2, p3, gain, upstream, *rest):
    count = 1 + max(entry[0] for entry in layout)
    weights = rest[:count]
    full, normed, scale, hid, gate_grad, up_grad = rest[count : count + 6]
    sums, sums_back = rest[count + 6 : count + 10], rest[count + 10 : count + 14]
    buffer, sems = rest[count + 14 :]
    copies = load_rows(weights, layout, spot, buffer, sems)
    join_feats(spot, (p0, p1, p2, p3), full)
    norm_rows(full, gain, normed, scale)
    for copy in copies:
        copy.wait()
    hidden = hid.shape[1]
    tile = 256
    for start in range(0, hidden, tile):
        here = slice(start, start + tile)
        g = dot(normed[...], buffer[:, here], 1, 0)
        u = dot(normed[...], buffer[:, hidden + start : hidden + start + tile], 1, 0)
        grad = dot(upstream[...], buffer[:, 2 * hidden + start : 2 * hidden + start + tile], 1, 0)
        sig = jax.nn.sigmoid(g)
        hid[:, here] = (g * sig * u).astype(LOW)
        gate_grad[:, here] = (grad * u * sig * (1.0 + g * (1.0 - sig))).astype(LOW)
        up_grad[:, here] = (grad * g * sig).astype(LOW)
    share = sums[0].shape[1]
    store_parts(
        sums_back,
        spot,
        lambda start: dot(gate_grad[...], buffer[pl.ds(start, share), :hidden], 1, 1)
        + dot(up_grad[...], buffer[pl.ds(start, share), hidden : 2 * hidden], 1, 1),
        share,
    )
    store_parts(
        sums,
        spot,
        lambda start: dot(hid[...], buffer[pl.ds(start, share), 2 * hidden : 3 * hidden], 1, 1),
        share,
    )


def ffn_back_body(finish, layout, spot, *rest):
    count = 1 + max(entry[0] for entry in layout)
    if finish:
        p0, p1, p2, p3, before_full, rows_full, scale, moved = rest[:8]
        rest = rest[8:]
    else:
        full_in = rest[0]
        rest = rest[1:]
    gate, up = rest[:2]
    weights = rest[2 : 2 + count]
    rest = rest[2 + count :]
    if finish:
        full, own = rest[:2]
        rest = rest[2:]
    gate_grad, up_grad, part0, part1, part2, part3, buffer, sems = rest
    copies = load_rows(weights, layout, spot, buffer, sems)
    if finish:
        finish_back(
            spot, (p0, p1, p2, p3), before_full, rows_full, scale, moved, full, own
        )
    else:
        full = full_in
    for copy in copies:
        copy.wait()
    hidden = gate.shape[1]
    tile = 256

    for start in range(0, hidden, tile):
        here = slice(start, start + tile)
        grad = dot(full[...], buffer[:, 2 * hidden + start : 2 * hidden + start + tile], 1, 0)
        g = gate[:, here].astype(F32)
        sig = jax.nn.sigmoid(g)
        gate_grad[:, here] = (
            grad * up[:, here].astype(F32) * sig * (1.0 + g * (1.0 - sig))
        ).astype(LOW)
        up_grad[:, here] = (grad * g * sig).astype(LOW)
    share = part0.shape[1]
    store_parts(
        (part0, part1, part2, part3),
        spot,
        lambda start: dot(gate_grad[...], buffer[pl.ds(start, share), :hidden], 1, 1)
        + dot(up_grad[...], buffer[pl.ds(start, share), hidden : 2 * hidden], 1, 1),
        share,
    )


def grad_columns(pairs, blocks, operands, rows, out, out_rows):
    col = 0
    for left, right in pairs:
        right = operands[right]
        width = right.shape[1]
        for start in range(0, width, 512):
            tile = min(512, width - start)
            out[out_rows, col : col + tile] = dot(
                blocks[left][:, rows], right[:, start : start + tile], 0, 0
            ).astype(LOW)
            col += tile


def arrange(operands, pairs, spot, order, scratch):
    blocks = {}
    for buffer, left in zip(scratch, sorted({left for left, _ in pairs})):
        width = buffer.shape[1] // len(order)
        for i, block in enumerate(order):
            at = pl.multiple_of(block(spot) * width, width)
            buffer[:, i * width : (i + 1) * width] = operands[left][:, pl.ds(at, width)]
        blocks[left] = buffer
    return blocks


def weight_grad_group_body(pairs, order, fit, spot, *refs):
    operands, (out,) = refs[: len(refs) - 1 - fit], refs[len(refs) - 1 - fit :][:1]
    blocks = arrange(operands, pairs, spot, order, refs[len(refs) - fit :]) if fit else operands
    step = min(256, out.shape[0])
    for start in range(0, out.shape[0], step):
        rows = slice(start, start + step)
        grad_columns(pairs, blocks, operands, rows, out, rows)


def relative_order(k):
    def bits(i):
        return [(i >> (k - 1 - j)) & 1 for j in range(k)]

    first = [(tuple(bits(i)), 0) for i in range(2**k)]
    second = [(tuple(reversed(bits(i))), 1) for i in range(2**k)]
    return first + second


def weight_grad_sent_body(pairs, order, fit, spot, *refs):
    operands, outs = refs[: len(refs) - 4 - fit], refs[len(refs) - 4 - fit :][:4]
    blocks = arrange(operands, pairs, spot, order, refs[len(refs) - fit :]) if fit else operands
    depth = outs[0].shape[0]
    for i, out in zip((1, 3, 0, 2), outs):
        rows = slice(i * depth, (i + 1) * depth)
        grad_columns(pairs, blocks, operands, rows, out, slice(0, depth))


def attend_back_body(
    slots, n_blocks, first_block, first, layout, spot, bias, queries, attended, logs, *rest
):
    count = 1 + max([entry[0] for entry in layout] + [-1])
    own_kinds, kinds, masks = rest[:3]
    blocks = rest[3 : 3 + n_blocks]
    rest = rest[3 + n_blocks :]
    tokens, width = queries.shape
    if first:
        p0, p1, p2, p3, before_full, rows_full, scale, moved = rest[:8]
        weights = rest[8 : 8 + count]
        full, own, out_grad, deltas, query_grad, same_sum = rest[8 + count : 14 + count]
        grads = rest[14 + count : 14 + count + n_blocks]
        buffer, sems = rest[14 + count + n_blocks :]
        copies = load_rows(weights, layout, spot, buffer, sems)
        finish_back(
            spot, (p0, p1, p2, p3), before_full, rows_full, scale, moved, full, own
        )
        for copy in copies:
            copy.wait()
        out_grad[...] = dot(full[...], buffer[:, 3 * width :], 1, 0).astype(LOW)
    else:
        out_grad, deltas, query_before = rest[:3]
        query_grad, same_sum = rest[3:5]
        grads = rest[5 : 5 + n_blocks]
    heads = width // HD
    size = tokens // slots
    wide = 2 * HD
    side = lax.broadcasted_iota(jnp.int32, (1, wide), 1) // HD
    if first:
        for head in range(heads):
            cols = slice(head // 2 * wide, (head // 2 + 1) * wide)
            product = attended[:, cols].astype(F32) * out_grad[:, cols].astype(F32)
            deltas[:, head : head + 1] = jnp.sum(
                jnp.where(side == head % 2, product, 0.0), axis=1, keepdims=True
            )
    same_sum[...] = jnp.zeros_like(same_sum)
    for slot in range(slots):
        keys = pl.ds(slot * size, size)
        for pair in range(heads // 2):
            cols = slice(pair * wide, (pair + 1) * wide)
            values = slice(width + pair * wide, width + (pair + 1) * wide)
            both = queries[keys, cols]
            grad_both = out_grad[keys, cols]
            query_total = None
            for b in range(n_blocks):
                place_b = first_block + b
                these = slice(place_b * size, (place_b + 1) * size)
                same = own_kinds[keys, :] == kinds[slot : slot + 1, these]
                k = blocks[b][keys, cols]
                v = blocks[b][keys, values]
                key_total = value_total = None
                for half in range(2):
                    head = 2 * pair + half
                    q = jnp.where(side == half, both, jnp.zeros_like(both))
                    g = jnp.where(side == half, grad_both, jnp.zeros_like(both))
                    step = bias[2 * head] - bias[2 * head + 1]
                    base = bias[2 * head + 1]
                    scores = scores_of(q, k, same, masks[slot : slot + 1, these] + base, step)
                    soft = jnp.exp(scores - logs[keys, head : head + 1])
                    soft_grad = dot(g, v, 1, 1)
                    score_grad = soft * (soft_grad - deltas[keys, head : head + 1])
                    same_sum[head : head + 1, :] += jnp.sum(
                        jnp.where(same, score_grad, 0.0), axis=0, keepdims=True
                    )
                    low = score_grad.astype(LOW)
                    masked_k = jnp.where(side == half, k, jnp.zeros_like(k))
                    query_part = dot(low, masked_k, 1, 0)
                    key_part = dot(low, q, 0, 0)
                    value_part = dot(soft.astype(LOW), g, 0, 0)
                    query_total = query_part if query_total is None else query_total + query_part
                    key_total = key_part if key_total is None else key_total + key_part
                    value_total = value_part if value_total is None else value_total + value_part
                grads[b][keys, cols] = key_total.astype(grads[b].dtype)
                grads[b][keys, values] = value_total.astype(grads[b].dtype)
            query_total = query_total * 0.125
            if not first:
                query_total = query_total + query_before[keys, cols]
            query_grad[keys, cols] = query_total


def qkv_back_body(layout, n_received, spot, query_grad, key_value, cosine, sine, *rest):
    count = 1 + max(entry[0] for entry in layout)
    received = rest[:n_received]
    weights = rest[n_received : n_received + count]
    three, part0, part1, part2, part3, buffer, sems = rest[n_received + count :]
    copies = load_rows(weights, layout, spot, buffer, sems)
    width = query_grad.shape[1]
    total = key_value[...]
    for other in received:
        total = total + other[...].astype(F32)
    three[:, :width] = turn(query_grad[...], cosine[...], -sine[...]).astype(LOW)
    three[:, width : 2 * width] = turn(total[:, :width], cosine[...], -sine[...]).astype(LOW)
    three[:, 2 * width :] = total[:, width:].astype(LOW)
    for copy in copies:
        copy.wait()
    share = part0.shape[1]
    store_parts(
        (part0, part1, part2, part3),
        spot,
        lambda start: dot(three[...], buffer[pl.ds(start, share), : 3 * width], 1, 1),
        share,
    )


def frame_body(slots, masked_rows, table, spot, mine, other, *rest):
    valid, full = (rest[0], rest[1]) if masked_rows else (None, rest[0])
    positions = mine.shape[2]
    blocks = table.shape[0]
    lanes = full.shape[1] // blocks
    for near in range(2):
        source = mine if near == 0 else other
        for slot in range(slots):
            start = pl.multiple_of((2 * slot + (spot[0] ^ near)) * positions, positions)
            for spot_out in range(blocks):
                block = table[spot_out]
                per = blocks // 4
                quarter = block // per
                which = (2 * ((quarter // 2) ^ spot[2])) + ((quarter % 2) ^ spot[1])
                lane = pl.multiple_of((block % per) * lanes, lanes)
                values = source[which, slot, :, pl.ds(lane, lanes)]
                if masked_rows:
                    values = values * valid[pl.ds(start, positions), :].astype(LOW)
                full[pl.ds(start, positions), spot_out * lanes : (spot_out + 1) * lanes] = values


def after(value, *others):
    return lax.optimization_barrier((value, others))[0]


def take_rows(place, natural, other):
    same = (place.c == place.zh).astype(jnp.int32)
    kept = pick(same, natural, other)
    received = place.swap_core(pick(same, other, natural))
    return pick(same, kept, received), pick(same, received, kept)


def return_rows(place, first, second):
    same = (place.c == place.zh).astype(jnp.int32)
    kept = pick(same, first, second)
    received = place.swap_core(pick(same, second, first))
    return pick(same, kept, received), pick(same, received, kept)


def gather_rows_swap(place, both, waits=()):
    k = len(place.dp)
    pieces, layout, early = [], [], []
    count = both[0].shape[0]
    for side, order in ((0, list(range(k))), (1, list(reversed(range(k))))):
        held, blocks = [both[side]], [(0,) * k]
        for index in order:
            send = held[0] if len(held) == 1 else jnp.concatenate(after(held, *waits), 0)
            held.append(place.swap_dp(send, index))
            if len(held) == 2:
                early.append(held[1])
            blocks += [b[:index] + (1 - b[index],) + b[index + 1 :] for b in blocks]
        at = 0
        for piece in held:
            for row in range(0, piece.shape[0], count):
                target = row_block(place, blocks[at], side)
                layout.append(
                    (
                        len(pieces),
                        lambda spot, row=row: row,
                        count,
                        lambda spot, target=target: target(spot) * count,
                        0,
                    )
                )
                at += 1
            pieces.append(piece)
    return pieces, layout, early


def row_block(place, bits, side):
    away_s, away_o = place.away(bits)
    chips = place.n_o
    return lambda spot: (
        ((spot[3] ^ away_s) * chips + (spot[4] ^ away_o)) * 2 + (spot[2] ^ side)
    )


def gather_rows_group(place, chunks):
    both = jnp.concatenate(
        [jnp.concatenate([chunk[side] for chunk in chunks], 1) for side in range(2)], 0
    )
    rows = lax.all_gather(both, ("shard", "o"), axis=0, tiled=True)
    chips = place.n_shard * place.n_o
    count = rows.shape[0] // (2 * chips)
    layout = [
        (
            0,
            lambda spot, i=i: i * count,
            count,
            lambda spot, i=i: (i - i % 2 + (i % 2 ^ spot[2])) * count,
            0,
        )
        for i in range(2 * chips)
    ]
    return [rows], layout


def join_chunks(*chunks):
    arrays, layout, column = [], [], 0
    for pieces, lay in chunks:
        layout += [(a + len(arrays), row, count, target, column) for a, row, count, target, _ in lay]
        arrays = arrays + pieces
        column += pieces[0].shape[1]
    return arrays, layout


def scatter_rows_group(place, partial):
    rows = lax.psum_scatter(partial, ("shard", "o"), scatter_dimension=0, tiled=True)
    half = rows.shape[0] // 2
    return rows[:half], rows[half:]


def scatter_start(place, sent, other_sent):
    return place.swap_dp(sent, 0), place.swap_dp(other_sent, len(place.dp) - 1)


def scatter_next(place, received, kept, step):
    k = len(place.dp)
    parts = [(a.astype(F32) + b.astype(F32)).astype(LOW) for a, b in zip(kept, received)]
    if step == k:
        return parts, None
    middle = parts[0].shape[0] // 2
    got = [
        place.swap_dp(parts[0][middle:], step),
        place.swap_dp(parts[1][middle:], k - 1 - step),
    ]
    return got, [part[:middle] for part in parts]


def scatter_rest(place, received, kept, step=1):
    while kept is not None:
        received, kept = scatter_next(place, received, kept, step)
        step += 1
    return received


def gather_feats(place, share):
    other = place.swap_zl(share)
    return [share, other, place.swap_core(share), place.swap_core(other)]


def scatter_feats(place, parts, beside=None):
    kept, kept_pair, sent, sent_pair = parts
    middle = (kept_pair.astype(F32) + place.swap_core(sent_pair).astype(F32)).astype(LOW)
    near = kept.astype(F32) + place.swap_core(sent).astype(F32)
    received = place.swap_zl(middle)
    done = None if beside is None else beside(middle)
    return near + after(received, done).astype(F32), done


def gather_keys(place, own):
    pieces = [own]
    for index in reversed(range(place.s_bits, len(place.dp))):
        pieces = pieces + [place.swap_dp(piece, index) for piece in pieces]
    return pieces


def per_device(place):
    def run(
        inputs,
        w_query,
        w_key,
        w_value,
        w_out,
        w_gate,
        w_up,
        w_down,
        attn_gain,
        ffn_gain,
        variate_bias,
        lengths,
        variates,
        cotangent,
    ):
        place.locate()
        positions, slots, quarter = inputs.shape
        depth = quarter * 4
        half_slots = slots // 2
        block = 2 * positions
        n_o = place.n_ctx // 2
        tokens = half_slots * block
        width = w_query.shape[2]
        heads = width // HD
        hidden = w_gate.shape[2]
        own_quarter = 2 * place.c + place.zl
        spot = jnp.stack([place.c, place.zl, place.zh, place.s, place.o]).astype(jnp.int32)
        k = len(place.dp)
        n_blocks = 2 ** (k + 1)
        block_rows = depth // n_blocks
        table = jnp.arange(n_blocks, dtype=jnp.int32)
        block_rows = depth // n_blocks
        lanes_fit = block_rows % 128 == 0

        attn_packs = [
            jnp.concatenate([w_query[i], w_key[i], w_value[i], w_out[i].T], 1)
            for i in range(LAYERS)
        ]

        def swap_slots(natural):
            first, second = natural[:, :half_slots], natural[:, half_slots:]
            return place.swap_zh(pick(place.zh, first, second).transpose(1, 0, 2))

        def two_quarters(natural, received):
            first, second = natural[:, :half_slots], natural[:, half_slots:]
            own = pick(place.zh, second, first).transpose(1, 0, 2)
            return jnp.stack([own, received])

        def four_quarters(two, other):
            return jnp.stack([two, other], 1).reshape(4, half_slots, positions, quarter)

        def token_rows(quarters, valid):
            mine, other = quarters[:2]
            if lanes_fit:
                operands = [table, spot, mine, other] + ([] if valid is None else [valid])
                return launch(
                    functools.partial(frame_body, half_slots, valid is not None),
                    [shape((tokens, depth), LOW)],
                    operands,
                    [SMEM, SMEM] + [VMEM] * (len(operands) - 2),
                    name="frame",
                )[0]
            by_core = jnp.stack([pick(place.c, other, mine), pick(place.c, mine, other)], 0)
            cut = by_core.reshape(2, 2, 2, half_slots, positions, quarter)
            cut = flip_if(place.zl, flip_if(place.zh, cut, 1), 2)
            rows = cut.transpose(3, 0, 4, 1, 2, 5).reshape(tokens, depth)
            return rows if valid is None else rows * valid.astype(LOW)

        def leave_rows(rows):
            cut = rows.reshape(half_slots, 2, positions, quarter)
            same = (place.c == place.zh).astype(jnp.int32)
            kept = pick(place.c, cut[:, 1], cut[:, 0])
            other = place.swap_core(pick(place.c, cut[:, 0], cut[:, 1]))
            mine = pick(same, kept, other)
            received = place.swap_zh(pick(same, other, kept))
            both = jnp.concatenate(
                [pick(place.zh, received, mine), pick(place.zh, mine, received)], 0
            )
            return both.transpose(1, 0, 2)

        zh_done = swap_slots(inputs)
        two = two_quarters(inputs, zh_done)
        zl_done = place.swap_zl(two)
        mine = four_quarters(two, zl_done)
        other = place.swap_core(mine)
        small = jnp.concatenate(
            [attn_gain.reshape(-1), ffn_gain.reshape(-1), variate_bias.reshape(-1)]
        ).reshape(1, -1)
        small = after(small, zh_done)
        pair = jnp.stack([small, place.swap_zh(small)], 0)
        all_small = jnp.stack([pair, place.swap_zl(pair)], 2)
        all_small = flip_if(place.zl, flip_if(place.zh, all_small, 0), 2)
        small = all_small.reshape(4, -1)
        cut = LAYERS * quarter
        natural_gains = jnp.concatenate(
            [
                small[:, i * cut : (i + 1) * cut]
                .reshape(4, LAYERS, quarter)
                .transpose(1, 0, 2)
                .reshape(LAYERS, depth)
                for i in range(2)
            ]
        )
        gains = natural_gains
        biases = lax.dynamic_index_in_dim(
            small[:, 2 * cut :].reshape(4, LAYERS, 2 * heads), own_quarter, 0, keepdims=False
        )

        ffn_chunks = [(w_gate[i], w_up[i], w_down[i].T) for i in range(LAYERS)]

        def take_late(natural, start, use):
            natural = after(natural, start)
            return take_rows(place, natural, after(place.swap_zh(natural), use))

        attn_both = take_late(attn_packs[0], zh_done, zh_done)
        gate = after(ffn_chunks[0][0], attn_both)
        gate_other = place.swap_zh(gate)
        *first_attn, early = gather_rows_swap(place, attn_both)
        up = after(ffn_chunks[0][1], early)
        up_other = place.swap_zh(up)

        own_kinds = after(variates.astype(F32), zl_done)
        rest = place.swap_core(own_kinds)
        own_kinds = jnp.concatenate(
            [pick(place.c, rest, own_kinds), pick(place.c, own_kinds, rest)], 0
        )
        own_kinds = pick(place.zh, own_kinds[:, half_slots:], own_kinds[:, :half_slots]).T
        kinds = jnp.concatenate(gather_keys(place, own_kinds), 1)
        own_kinds = own_kinds.reshape(tokens, 1)
        own_lengths = pick(place.zh, lengths[half_slots:], lengths[:half_slots])
        own_positions = place.o * block + jnp.arange(block, dtype=jnp.int32)
        chips = jnp.arange(n_o, dtype=jnp.int32) ^ place.o
        key_positions = (
            chips[:, None] * block + jnp.arange(block, dtype=jnp.int32)[None, :]
        ).reshape(-1)
        masks = jnp.where(key_positions[None, :] < own_lengths[:, None], 0.0, masked).astype(F32)
        valid = (own_positions[None, :] < own_lengths[:, None]).astype(F32).reshape(tokens, 1)
        index = jnp.arange(width, dtype=jnp.int32) % HD
        inverse = 10000.0 ** (-(2.0 * (index % (HD // 2)).astype(F32)) / HD)
        angles = own_positions.astype(F32)[:, None] * inverse[None, :]
        cosine = jnp.tile(jnp.cos(angles), (half_slots, 1))
        sine = jnp.tile(
            jnp.where(index < HD // 2, -1.0, 1.0)[None, :] * jnp.sin(angles), (half_slots, 1)
        )

        def share_of(rows):
            return lax.dynamic_slice_in_dim(rows, own_quarter * quarter, quarter, -1)

        attn_buffer = [
            pltpu.VMEM((depth, 4 * width), LOW),
            pltpu.SemaphoreType.DMA((n_blocks,)),
        ]
        ffn_buffer = [
            pltpu.VMEM((depth, 3 * hidden), LOW),
            pltpu.SemaphoreType.DMA((2 * n_blocks,)),
        ]
        rows_low = shape((tokens, depth), LOW)
        column = shape((tokens, 1), F32)
        share_f32 = shape((tokens, quarter), F32)
        parts = part_shapes(tokens, quarter)

        if lanes_fit:
            full = launch(
                functools.partial(frame_body, half_slots, False),
                [rows_low],
                [table, spot, mine, other],
                [SMEM, SMEM, VMEM, VMEM],
                name="frame",
            )[0]
        else:
            by_core = jnp.stack([pick(place.c, other, mine), pick(place.c, mine, other)], 0)
            cut4 = by_core.reshape(2, 2, 2, half_slots, positions, quarter)
            cut4 = flip_if(place.zl, flip_if(place.zh, cut4, 1), 2)
            full = cut4.transpose(3, 0, 4, 1, 2, 5).reshape(tokens, depth)

        pieces = [full]
        current = share_of(full).astype(F32)
        kept, weights = [], []
        attn_w, attn_lay = first_attn
        nothing = ()
        for layer in range(LAYERS):
            first, more = layer == 0, layer + 1 < LAYERS
            outs = launch(
                functools.partial(qkv_body, attn_lay, layer == 0),
                ([] if layer == 0 else [rows_low])
                + [
                    rows_low,
                    column,
                    shape((tokens, width), LOW),
                    shape((tokens, 2 * width), LOW),
                ],
                [spot, *pieces, gains[layer : layer + 1], cosine, sine, *attn_w],
                [SMEM] + [VMEM] * (3 + len(pieces)) + [HBM] * len(attn_w),
                attn_buffer,
                name="qkv",
            )
            if layer > 0:
                full, outs = outs[0], outs[1:]
            normed, scale, queries, key_value = outs
            blocks = gather_keys(place, key_value)
            if first:
                gate_both = take_rows(place, gate, after(gate_other, key_value))
                up_both = take_rows(place, up, after(up_other, key_value))
                down = after(ffn_chunks[0][2], key_value)
                down_other = place.swap_zh(down)
                blocks = after(blocks, down_other, gate_both, up_both)
                gate_up = gather_rows_group(place, after((gate_both, up_both), blocks))
            if layer == LAYERS - 1:
                late_cotangent = after(cotangent, key_value)
                late_other = swap_slots(late_cotangent)
                blocks = after(blocks, late_other)
                late_two = two_quarters(after(late_cotangent, blocks), late_other)
                late_other = place.swap_zl(late_two)
            if more:
                attn_next = after(attn_packs[layer + 1], blocks)
                attn_other = place.swap_zh(attn_next)
            attended, logs, *sums = launch(
                functools.partial(attend_body, half_slots, n_o, attn_lay),
                [shape((tokens, width), LOW), shape((tokens, heads), F32), *parts],
                [spot, biases[layer], queries, own_kinds, kinds, masks, *blocks, *attn_w],
                [SMEM] * 2 + [VMEM] * (4 + n_o) + [HBM] * len(attn_w),
                attn_buffer,
                name="attend",
            )
            if more:
                sums = after(sums, attn_other)
                chunks = ffn_chunks[layer + 1]
                others = [place.swap_zh(after(chunks[0], sums))]
            if first:
                down_both = take_rows(place, down, after(down_other, attended))

            if layer == LAYERS - 1:
                sums = after(sums, late_other)
                late_mine = four_quarters(late_two, after(late_other, sums))
                late_other = place.swap_core(late_mine)

            def reduce_side(sent):
                return list(others) if more else [late_other]

            shared, _ = scatter_feats(place, sums, reduce_side)
            middle = current + shared
            if first:
                down_w, down_lay, early = gather_rows_swap(place, down_both, (middle,))
            mid_pieces = gather_feats(place, middle.astype(LOW))
            if layer == LAYERS - 1:
                upstream_full = token_rows((after(late_mine, middle), late_other), valid)
                mid_pieces = after(mid_pieces, upstream_full)
            if more:
                others.append(place.swap_zh(after(chunks[1], middle)))
                attn_both = take_rows(place, attn_next, after(attn_other, middle))
                mid_pieces = after(mid_pieces, others[1], attn_both)
            if first:
                mid_pieces = after(mid_pieces, down_w)
                ffn_w, ffn_lay = join_chunks(gate_up, (down_w, down_lay))
            if more:
                others.append(place.swap_zh(after(chunks[2], mid_pieces)))
                next_w, next_lay, early = gather_rows_swap(
                    place, after(attn_both, mid_pieces, ffn_w), nothing
                )
            operands = [
                spot,
                *mid_pieces,
                gains[LAYERS + layer : LAYERS + layer + 1],
            ]
            specs = [SMEM] + [VMEM] * 5
            hidden_low = shape((tokens, hidden), LOW)
            if more:
                full_mid, normed_mid, scale_mid, gate, up, hid, *sums = launch(
                    functools.partial(ffn_body, ffn_lay),
                    [rows_low, rows_low, column, *[hidden_low] * 3, *parts],
                    [*operands, *ffn_w],
                    specs + [HBM] * len(ffn_w),
                    ffn_buffer,
                    name="ffn",
                )
            else:
                full_mid, normed_mid, scale_mid, hid, *outs = launch(
                    functools.partial(ffn_both_body, ffn_lay),
                    [rows_low, rows_low, column, *[hidden_low] * 3, *parts, *parts],
                    [*operands, upstream_full, *ffn_w],
                    specs + [VMEM] + [HBM] * len(ffn_w),
                    ffn_buffer,
                    name="ffn_both",
                )
                gate = up = None
                last_grads, sums, last_sums = outs[:2], outs[2:6], outs[6:]
            weights.append((attn_w, attn_lay, ffn_w, ffn_lay))
            if more:
                sums = after(sums, early, others[2])

            def take_side(sent):
                return [
                    take_rows(place, chunk, after(other, sent))
                    for chunk, other in zip(chunks, others)
                ]

            shared, ffn_both = scatter_feats(place, sums, take_side if more else None)
            if more:
                attn_w, attn_lay = next_w, next_lay
                ffn_w, ffn_lay = gather_rows_group(place, ffn_both)
            current = middle + shared
            kept.append(
                (
                    full,
                    normed,
                    scale,
                    queries,
                    blocks,
                    attended,
                    logs,
                    full_mid,
                    normed_mid,
                    scale_mid,
                    gate,
                    up,
                    hid,
                )
            )
            if more:
                pieces = gather_feats(place, current.astype(LOW))

        natural_valid = (
            ((2 * place.o + place.c) * positions + jnp.arange(positions, dtype=jnp.int32))[:, None]
            < lengths[None, :]
        )

        upstream = share_of(upstream_full).astype(F32)

        def step_back(sums, full_rows, row_scale, gain, before, beside, final=None):
            shared, done = scatter_feats(place, sums, beside)
            own_rows = share_of(full_rows).astype(F32) * row_scale
            gain_grad = jnp.sum(shared * own_rows, 0)
            part = shared * share_of(gain)[None, :]
            moved = before + row_scale * part
            if final:
                dots = jnp.sum(part * own_rows, 1)
                sums = final(gain_grad)
                other = place.swap_zl(jnp.concatenate([dots, sums]))
                dots = dots + other[:tokens]
                sums = jnp.stack([sums, other[tokens:]])
                other = place.swap_core(jnp.concatenate([dots, sums.reshape(-1)]))
                dots = (dots + other[:tokens]).reshape(tokens, 1) * (1.0 / depth)
                sums = jnp.stack([sums, other[tokens:].reshape(sums.shape)])
                sums = flip_if(place.c, flip_if(place.zl, sums, 1), 0)
                return moved, [moved - row_scale * own_rows * dots], sums, done
            return moved, gather_feats(place, moved.astype(LOW)), gain_grad, done

        sent_order = [row_block(place, bits, side) for bits, side in relative_order(k)]
        group_order = [
            lambda spot, i=i: i - i % 2 + (i % 2 ^ spot[2]) for i in range(n_blocks)
        ]

        def weight_grads_of(swapped, pairs, operands, columns, name, ready):
            operands = after(operands, ready)
            lefts = sorted({left for left, _ in pairs})
            order = sent_order if swapped else group_order
            scratch = []
            if lanes_fit:
                scratch = [pltpu.VMEM((tokens, depth), LOW) for _ in lefts]
            else:
                index = jnp.stack([block(spot) for block in order])
                operands = [
                    jnp.take(array.reshape(tokens, n_blocks, block_rows), index, axis=1).reshape(
                        tokens, depth
                    )
                    if i in lefts
                    else array
                    for i, array in enumerate(operands)
                ]
            return launch(
                functools.partial(
                    weight_grad_sent_body if swapped else weight_grad_group_body,
                    pairs,
                    order,
                    len(scratch),
                ),
                [shape((depth // 4, columns), LOW)] * 4
                if swapped
                else [shape((depth, columns), LOW)],
                [spot, *operands],
                [SMEM] + [VMEM] * len(operands),
                scratch,
                name=name,
            )

        weight_grads = [None] * LAYERS

        def keep_grads(layer, ffn_out, attn_out):
            attn_out, ffn_out = attn_out.astype(F32), ffn_out.astype(F32)
            weight_grads[layer] = (
                attn_out[:, :width],
                attn_out[:, width : 2 * width],
                attn_out[:, 2 * width : 3 * width],
                attn_out[:, 3 * width :].T,
                ffn_out[:, :hidden],
                ffn_out[:, hidden : 2 * hidden],
                ffn_out[:, 2 * hidden :].T,
            )

        late = None
        gain_grads = [None] * LAYERS
        bias_grads = [None] * LAYERS
        half_keys = max(n_o // 2, 1)
        pending = None
        for layer in reversed(range(LAYERS)):
            attn_w, attn_lay, ffn_w, ffn_lay = weights[layer]
            (
                full,
                normed,
                scale,
                queries,
                blocks,
                attended,
                logs,
                full_mid,
                normed_mid,
                scale_mid,
                gate,
                up,
                hid,
            ) = kept[layer]
            hidden_low = shape((tokens, hidden), LOW)
            if pending is None:
                (gate_grad, up_grad), sums = last_grads, last_sums
            else:
                upstream_full, upstream, gate_grad, up_grad, *sums = launch(
                    functools.partial(ffn_back_body, True, ffn_lay),
                    [rows_low, share_f32, hidden_low, hidden_low, *parts],
                    [spot, *pending, gate, up, *ffn_w],
                    [SMEM] + [VMEM] * 10 + [HBM] * len(ffn_w),
                    ffn_buffer,
                    name="ffn_back",
                )
            if late is not None:
                late_ffn, late_got, late_kept = late
                sums = after(sums, late_got)
            ffn_grads = functools.partial(
                weight_grads_of,
                False,
                ((0, 1), (0, 2), (3, 4)),
                [normed_mid, gate_grad, up_grad, upstream_full, hid],
                3 * hidden,
                "ffn_weights",
            )

            def ffn_side(sent):
                partial = ffn_grads(sent)
                return after(partial, current) if late is None else partial

            moved, pieces, ffn_gain_grad, ffn_partial = step_back(
                sums, full_mid, scale_mid, gains[LAYERS + layer], upstream, ffn_side
            )
            ffn_rows = scatter_rows_group(place, *after(ffn_partial, moved))
            if late is not None:
                own_ffn, other_ffn = return_rows(place, *after(late_ffn, moved))
                late_got, late_kept = scatter_next(place, after(late_got, moved), late_kept, 1)
                pieces = after(pieces, other_ffn, late_kept)
                others = [place.swap_zh(after(other_ffn[:, :hidden], pieces))]
            common = [queries, attended, logs, own_kinds, kinds, masks]
            later = blocks[half_keys:] if n_o > 1 else blocks
            early = blocks[:half_keys] if n_o > 1 else []
            start = half_keys if n_o > 1 else 0
            middle_full, middle, out_grad, deltas, query_grad, same_sum, *sent = launch(
                functools.partial(
                    attend_back_body, half_slots, len(later), start, True, attn_lay
                ),
                [
                    rows_low,
                    share_f32,
                    shape((tokens, width), LOW),
                    shape((tokens, heads), F32),
                    shape((tokens, width), F32),
                    shape((heads, block), F32),
                    *[shape((tokens, 2 * width), LOW)] * len(later),
                ],
                [
                    spot,
                    biases[layer],
                    *common,
                    *later,
                    *pieces,
                    upstream_full,
                    full_mid,
                    scale_mid,
                    moved,
                    *attn_w,
                ],
                [SMEM] * 2 + [VMEM] * (6 + len(later) + 8) + [HBM] * len(attn_w),
                attn_buffer,
                name="attend_back_far",
            )
            if layer == LAYERS - 1:
                output = leave_rows(after(current, moved).astype(LOW))
                output = output * natural_valid[:, :, None].astype(LOW)
                out_grad = after(out_grad, output)
            if late is not None:
                out_grad = after(out_grad, others[0], late_got)
                others.append(place.swap_zh(after(other_ffn[:, hidden : 2 * hidden], out_grad)))
                late_ends = scatter_rest(place, after(late_got, out_grad), late_kept, 2)
                own_attn, other_attn = return_rows(place, *late_ends)
            query_grad, same_sum_near, *near = launch(
                functools.partial(attend_back_body, half_slots, len(early), 0, False, []),
                [
                    shape((tokens, width), F32),
                    shape((heads, block), F32),
                    *[shape((tokens, 2 * width), F32)] * len(early),
                ],
                [spot, biases[layer], *common, *early, out_grad, deltas, query_grad],
                [SMEM] * 2 + [VMEM] * (6 + len(early) + 3),
                name="attend_back_near",
            )
            same_total = jnp.sum(same_sum, 1) + jnp.sum(same_sum_near, 1)
            bias_grads[layer] = jnp.stack([same_total, -same_total], 1)
            received = [place.swap_dp(piece, place.s_bits) for piece in sent]
            for index in range(place.s_bits + 1, k):
                near = [a + b.astype(F32) for a, b in zip(near, received)]
                middle_at = len(near) // 2
                received = [
                    place.swap_dp(piece.astype(LOW), index) for piece in near[middle_at:]
                ]
                near = near[:middle_at]
            if late is not None:
                received = after(received, others[1], other_attn)
                others.append(place.swap_zh(after(other_ffn[:, 2 * hidden :], received)))
            three, *sums = launch(
                functools.partial(qkv_back_body, attn_lay, 1),
                [shape((tokens, 3 * width), LOW), *parts],
                [spot, query_grad, near[0], cosine, sine, received[0], *attn_w],
                [SMEM] + [VMEM] * 5 + [HBM] * len(attn_w),
                attn_buffer,
                name="qkv_back",
            )
            if late is not None:
                sums = after(sums, others[2])
                others.append(place.swap_zh(after(other_attn, sums)))
            attn_grads = functools.partial(
                weight_grads_of,
                True,
                ((0, 1), (2, 3)),
                [normed, three, middle_full, attended],
                4 * width,
                "attn_weights",
            )

            def small_sums(gain_grad):
                gain_grads[0] = (gain_grad, ffn_gain_grad)
                mine = [gain_grads[i][j] for j in range(2) for i in range(LAYERS)]
                return jnp.concatenate([*mine, jnp.stack(bias_grads).reshape(-1)])

            def attn_side(sent):
                partial = attn_grads(sent)
                if late is None:
                    return partial, None
                return after(partial, others[3]), None

            moved, pieces, attn_gain_grad, (attn_partial, last_rows) = step_back(
                sums, full, scale, gains[layer], middle, attn_side, small_sums if layer == 0 else None
            )
            pending = [*pieces, middle_full, full, scale, moved]
            gain_grads[layer] = (attn_gain_grad, ffn_gain_grad)
            if late is not None:
                last_own, last_other = return_rows(place, *after(ffn_rows, moved))
                pending[0] = after(pending[0], last_other)
                last_sent = place.swap_zh(after(last_other, moved))
                keep_grads(
                    layer + 1,
                    own_ffn.astype(F32) + jnp.concatenate(others[:3], 1).astype(F32),
                    own_attn.astype(F32) + others[3].astype(F32),
                )
            sent, other_sent, *attn_kept = after(attn_partial, moved)
            late = (ffn_rows, scatter_start(place, sent, other_sent), attn_kept)

        input_grad = leave_rows(pending[0].astype(LOW)).astype(F32)
        ends = scatter_rest(place, *after(late[1:], last_other))
        own_attn, other_attn = return_rows(place, *after(ends, last_sent))
        attn_out = own_attn.astype(F32) + place.swap_zh(other_attn).astype(F32)
        total = after(attn_gain_grad, other_attn)
        for i in range(k):
            total = total + place.swap_dp(total, i)
        total = total + place.swap_zh(total)
        small_cut = LAYERS * quarter
        total = total.reshape(4, -1)
        wide = total[:, : 2 * small_cut].reshape(4, 2 * LAYERS, quarter)
        bias_wide = total[:, 2 * small_cut :].reshape(4, LAYERS, heads, 2)
        ffn_out = last_own.astype(F32) + last_sent.astype(F32)
        keep_grads(0, ffn_out, attn_out)
        tensor = 2 * place.zh + place.zl
        gains_out = lax.dynamic_index_in_dim(wide, tensor, 0, keepdims=False)
        bias_out = lax.dynamic_index_in_dim(bias_wide, tensor, 0, keepdims=False)
        stacks = [
            jnp.stack([weight_grads[layer][member] for layer in range(LAYERS)])
            for member in range(7)
        ]
        return (output, input_grad, *stacks, gains_out[:LAYERS], gains_out[LAYERS:], bias_out)

    return run


def solution(mesh):
    n_ctx = mesh.shape["ctx"]
    dims = (mesh.shape["shard"], n_ctx // 2, 2, 2, mesh.shape["tensor"] // 2)
    mesh = jax.sharding.Mesh(mesh.devices.reshape(dims), AXES)
    ctx, tensor = ("o", "c"), ("zh", "zl")
    column = P(None, ("shard", "o", "c"), tensor)
    row = P(None, tensor, ("shard", "o", "c"))
    tokens = P(ctx, "shard", tensor)
    gain = P(None, tensor)
    bias = P(None, tensor, None)
    return jax.shard_map(
        per_device(Place(mesh)),
        mesh=mesh,
        in_specs=(
            tokens, column, column, column, row, column, column, row,
            gain, gain, bias, P("shard"), P(ctx, "shard"), tokens,
        ),
        out_specs=(
            tokens, tokens, column, column, column, row, column, column, row, gain, gain, bias,
        ),
        check_vma=False,
    )
```
